32 devices in a mesh: lat: 4 (over x, core), lon: 8 (over z, y).
Axes of the slice: x: 2, y: 2, z: 4, core: 2. Of those that a mesh axis runs over, the one named last changes fastest.
Arguments:
- probe_signs: int32 [16, 1024, 512], P(None, 'lon', 'lat'), may hold values from -1 to 1, as said below
- ocean_mask: int32 [1024, 512], P('lon', 'lat'), may hold values 0 or 1
- kappa_sq: float32 [1024, 512], P('lon', 'lat'), may hold values from 0.02 to 0.5
- block_ids: int32 [1024, 512], P('lon', 'lat'), may hold values from 0 to 63
Outputs:
- solution: float32 [16, 1024, 512], P(None, 'lon', 'lat')
- trace_terms: float32 [16, 1024, 512], P(None, 'lon', 'lat')
- traces: float32 [16, 64], replicated
The draws below stay inside these ranges and needn't reach their ends.
Inputs may be any that keep to these rules, and one draw needn't show every extreme that they name: `probe_signs`: each entry is -1 or +1.
All inputs are finite; a program needn't handle non-finite values. No bound on the sum of `ocean_mask` on one device may be relied on, other than what follows from the above.
Results may differ from the reference program's by a relative error of at most 0.0003.
Values sent between devices are 32-bit elements; how exact they have to be, the bound alone decides.
A program may use at most 64 MiB of HBM per device.

```python
import math
import jax
import jax.numpy as jnp

PROBES = 16
ITERS = 3
NB = 64
NLAT = 512
NLON = 1024


def draw_probe_signs(key, part):
    return 2 * jax.random.randint(key, (PROBES, NLON, NLAT), 0, 2, dtype=jnp.int32) - 1


def set_ends(array, stream_key, least, top_value):
    longest = array.shape.index(max(array.shape))
    spots = []
    for shift in (0, 1):
        where = [jax.random.randint(jax.random.fold_in(stream_key, axis), (), 0, length) for axis, length in enumerate(array.shape)]
        where[longest] = (where[longest] + shift) % array.shape[longest]
        spots.append(tuple(where))
    return array.at[spots[0]].set(least).at[spots[1]].set(top_value)


def block_scale(key, dims, shards, least, largest):
    level = 1.0
    for dim, shards_of in shards:
        draws = jax.random.uniform(jax.random.fold_in(jax.random.fold_in(key, 6), dim), (shards_of,), jnp.float32, least / len(shards), largest / len(shards))
        level = level * jnp.repeat(jnp.exp(draws), dims[dim] // shards_of).reshape((-1,) + (1,) * (len(dims) - 1 - dim))
    return level


def setup_inputs(seed: int = 0) -> dict:
    keys = jax.random.split(jax.random.key(seed), 5)
    probe_signs = draw_probe_signs(jax.random.fold_in(keys[4], 71), 0)
    ocean_mask = set_ends((jax.random.randint(keys[1], (NLON, NLAT), 0, 4) < 3).astype(jnp.int32), jax.random.fold_in(keys[1], 1), 0, 1)
    kappa_sq = jnp.clip(jnp.exp(math.log(0.5) - 3.218876 * jax.random.uniform(keys[2], (NLON, NLAT), jnp.float32) ** block_scale(keys[2], (NLON, NLAT), ((0, 8), (1, 4)), -0.2, 0.2)), 0.02, 0.5)
    block_ids = set_ends(jax.random.randint(keys[3], (NLON, NLAT), 0, NB), jax.random.fold_in(keys[3], 1), 0, NB - 1).astype(jnp.int32)
    return {"probe_signs": probe_signs, "ocean_mask": ocean_mask, "kappa_sq": kappa_sq, "block_ids": block_ids}


def operate(field, kappa_sq, ocean_mask):
    padded = jnp.pad(field, ((0, 0), (0, 0), (1, 1)))
    total = jnp.roll(field, 1, axis=1) + jnp.roll(field, -1, axis=1)
    total = total + padded[:, :, :-2] + padded[:, :, 2:]
    return ocean_mask * ((kappa_sq + 0.25) * field - 0.0625 * total)


def reference(probe_signs, ocean_mask, kappa_sq, block_ids):
    ocean_float = ocean_mask.astype(jnp.float32)
    probes = probe_signs.astype(jnp.float32) * ocean_float
    solution = jnp.zeros_like(probes)
    residual = probes
    direction = probes
    norm_now = jnp.sum(residual * residual, axis=(1, 2))
    for turn_index in range(ITERS):
        image = operate(operate(direction, kappa_sq, ocean_float), kappa_sq, ocean_float)
        alpha = norm_now / jnp.sum(direction * image, axis=(1, 2))
        solution = solution + alpha[:, None, None] * direction
        residual = residual - alpha[:, None, None] * image
        norm_next = jnp.sum(residual * residual, axis=(1, 2))
        direction = residual + (norm_next / norm_now)[:, None, None] * direction
        norm_now = norm_next
    applied_sol = operate(solution, kappa_sq, ocean_float)
    applied_probe = operate(probes, kappa_sq, ocean_float)
    trace_estimate = kappa_sq * (solution * applied_probe + applied_sol * probes)
    reduced_total = jax.ops.segment_sum(trace_estimate.reshape(PROBES, -1).T, block_ids.reshape(-1).astype(jnp.int32), num_segments=NB)
    traces = reduced_total.T / jnp.float32(NLAT * NLON // NB)
    return solution, trace_estimate, traces
```

```python
import jax
import jax.numpy as jnp
from jax import lax
from jax.sharding import PartitionSpec as P

NB = 64
WIDTH = 5
SHIFTS = (0.2, 0.4)
FLOOR = 1e-6


def extended(cells, axis, dim, width, closed):
    count = lax.axis_size(axis)
    ends = count if closed else count - 1
    head = lax.slice_in_dim(cells, 0, width, axis=dim)
    tail = lax.slice_in_dim(cells, cells.shape[dim] - width, cells.shape[dim], axis=dim)
    before = lax.ppermute(tail, axis, [(i, (i + 1) % count) for i in range(ends)])
    after = lax.ppermute(head, axis, [((i + 1) % count, i) for i in range(ends)])
    return jnp.concatenate([before, cells, after], axis=dim)


def stencil(field, centre, side):
    total = field[:, :-2, 1:-1] + field[:, 2:, 1:-1]
    total = total + field[:, 1:-1, :-2] + field[:, 1:-1, 2:]
    return centre * field[:, 1:-1, 1:-1] - side * total


def weights(gram, right):
    g00, g01, g02, g11, g12, g22 = gram
    r0, r1, r2 = right
    l10 = g01 / g00
    l20 = g02 / g00
    d1 = g11 - l10 * g01
    e12 = g12 - l10 * g02
    ok1 = d1 > FLOOR * g11
    i1 = jnp.where(ok1, 1.0 / jnp.where(ok1, d1, 1.0), 0.0)
    l21 = e12 * i1
    d2 = g22 - l20 * g02 - l21 * e12
    ok2 = d2 > FLOOR * g22
    i2 = jnp.where(ok2, 1.0 / jnp.where(ok2, d2, 1.0), 0.0)
    z0 = r0
    z1 = r1 - l10 * z0
    z2 = r2 - l20 * z0 - l21 * z1
    y2 = z2 * i2
    y1 = z1 * i1 - l21 * y2
    y0 = z0 / g00 - l10 * y1 - l20 * y2
    return y0, y1, y2


def per_device(probe_signs, ocean_mask, kappa_sq, block_ids):
    probes = probe_signs.astype(jnp.float32) * ocean_mask.astype(jnp.float32)
    planes = jnp.concatenate([probes, kappa_sq[None]], axis=0)
    planes = extended(planes, "lon", 1, WIDTH, True)
    planes = extended(planes, "lat", 2, WIDTH, False)
    wide, wide_kappa = planes[:-1], planes[-1]
    ocean = wide[0] * wide[0]
    centre = ocean * (wide_kappa + 0.25)
    side = 0.0625 * ocean

    def cut(field, width):
        return field[..., width:field.shape[-2] - width, width:field.shape[-1] - width]

    v0 = wide
    w0 = stencil(v0, cut(centre, 1), cut(side, 1))
    v1 = stencil(w0, cut(centre, 2), cut(side, 2)) - SHIFTS[0] * cut(v0, 2)
    w1 = stencil(v1, cut(centre, 3), cut(side, 3))
    v2 = stencil(w1, cut(centre, 4), cut(side, 4)) - SHIFTS[1] * cut(v1, 2)
    w2 = stencil(v2, cut(centre, 5), cut(side, 5))
    v0, w0, v1, w1, v2 = (cut(f, n) for f, n in ((v0, 5), (w0, 4), (v1, 3), (w1, 2), (v2, 1)))

    def dot(a, b):
        return jnp.sum(a * b, axis=(1, 2))

    dots = jnp.stack([
        dot(w0, w0), dot(w0, w1), dot(w0, w2), dot(w1, w1), dot(w1, w2), dot(w2, w2),
        dot(v0, v0), dot(v0, v1), dot(v0, v2),
    ])
    terms = [kappa_sq * (v * w0 + w * v0) for v, w in ((v0, w0), (v1, w1), (v2, w2))]
    indicator = (
        block_ids[:, :, None] == jnp.arange(NB, dtype=jnp.int32)[None, None, :]
    ).astype(jnp.float32)
    sums = jnp.einsum(
        "szt,zti->si", jnp.concatenate(terms, axis=0), indicator, precision=lax.Precision.HIGHEST
    )
    count = probes.shape[0]
    both = jnp.concatenate([dots.reshape(-1), sums.reshape(-1)])
    both = lax.psum(both, ("lat", "lon"))
    dots = both[:9 * count].reshape(9, count)
    sums = both[9 * count:].reshape(3, count, NB)
    y = weights(tuple(dots[:6]), tuple(dots[6:]))
    yf = [a[:, None, None] for a in y]
    solved = yf[0] * v0 + yf[1] * v1 + yf[2] * v2
    trace = yf[0] * terms[0] + yf[1] * terms[1] + yf[2] * terms[2]
    cells_total = (
        kappa_sq.shape[0] * kappa_sq.shape[1] * lax.axis_size("lat") * lax.axis_size("lon")
    )
    traces = sum(a[:, None] * s for a, s in zip(y, sums)) / jnp.float32(cells_total // NB)
    return solved, trace, traces


def solution(mesh):
    placed = (P(None, "lon", "lat"), P("lon", "lat"), P("lon", "lat"), P("lon", "lat"))
    return jax.shard_map(
        per_device,
        mesh=mesh,
        in_specs=placed,
        out_specs=(P(None, "lon", "lat"), P(None, "lon", "lat"), P()),
        check_vma=False,
    )
```

```python
import functools

import jax
import jax.numpy as jnp
from jax import lax
from jax.experimental import pallas as pl
from jax.experimental.pallas import tpu as pltpu
from jax.sharding import PartitionSpec as P

NB = 64
EDGE = 7
PAD = 8
SHIFT = 0.4
FLOOR = 1e-6
CHUNK = 48
MESH = pl.DeviceIdType.MESH


def weights(gram, right):
    g00, g01, g02, g11, g12, g22 = gram
    r0, r1, r2 = right
    l10 = g01 / g00
    l20 = g02 / g00
    d1 = g11 - l10 * g01
    e12 = g12 - l10 * g02
    ok1 = d1 > FLOOR * g11
    i1 = jnp.where(ok1, 1.0 / jnp.where(ok1, d1, 1.0), 0.0)
    l21 = e12 * i1
    d2 = g22 - l20 * g02 - l21 * e12
    ok2 = d2 > FLOOR * g22
    i2 = jnp.where(ok2, 1.0 / jnp.where(ok2, d2, 1.0), 0.0)
    z1 = r1 - l10 * r0
    z2 = r2 - l20 * r0 - l21 * z1
    y2 = z2 * i2
    y1 = z1 * i1 - l21 * y2
    y0 = r0 / g00 - l10 * y1 - l20 * y2
    return y0, y1, y2


def kernel(
    nlat, nlon, signs, mask, kappa, ids, solved, trace, traces,
    planes, halo, left_edge, right_edge, coef, work, kept, terms, dots, ys,
    gram_lat, gram_lon, sums_lat, sums_lon,
    halo_send, halo_recv, lat_send, lat_recv, lon_send, lon_recv,
):
    count, rows, lanes = signs.shape
    ext = rows + 2 * PAD
    lat, lon = lax.axis_index("lat"), lax.axis_index("lon")
    up, down = lax.rem(lon + 1, nlon), lax.rem(lon + nlon - 1, nlon)

    barrier = pltpu.get_barrier_semaphore()
    for d in range(1, nlat):
        pl.semaphore_signal(
            barrier, inc=1, device_id=(lax.rem(lat + d, nlat), lon), device_id_type=MESH)
    for d in range(1, nlon):
        pl.semaphore_signal(
            barrier, inc=1, device_id=(lat, lax.rem(lon + d, nlon)), device_id_type=MESH)

    lane = lax.broadcasted_iota(jnp.int32, (1, lanes), 1)

    def pack(step, carry):
        part = pl.ds(pl.multiple_of(step * 32, 32), 32)
        ocean = mask[part, :].astype(jnp.float32)
        first = jnp.zeros((32, lanes), jnp.float32)
        last = jnp.zeros((32, lanes), jnp.float32)
        for p in range(count + 1):
            if p < count:
                x = signs[p, part, :].astype(jnp.float32) * ocean
            else:
                x = kappa[part, :]
            planes[p, pl.ds(pl.multiple_of(step * 32 + PAD, 8), 32), :] = x
            here = (lane >= EDGE * p) & (lane < EDGE * (p + 1))
            first = jnp.where(here, pltpu.roll(x, EDGE * p, 1) if p else x, first)
            last = jnp.where(here, pltpu.roll(x, EDGE * (p + 1), 1), last)
        left_edge[part, :] = first
        right_edge[part, :] = last
        return carry

    lax.fori_loop(0, rows // 32, pack, 0)
    pl.semaphore_wait(barrier, nlat + nlon - 2)

    def copy(src, dst, k, device):
        return pltpu.make_async_remote_copy(
            src_ref=src, dst_ref=dst, send_sem=halo_send.at[k], recv_sem=halo_recv.at[k],
            device_id=device, device_id_type=MESH)

    own = pl.ds(PAD, rows)
    top, low = pl.ds(rows, PAD), pl.ds(PAD, PAD)
    before, after = pl.ds(0, PAD), pl.ds(rows + PAD, PAD)
    go_right = copy(right_edge, halo.at[0, own, :], 0, (lax.min(lat + 1, nlat - 1), lon))
    go_left = copy(left_edge, halo.at[1, own, :], 1, (lax.max(lat - 1, 0), lon))
    go_up = copy(planes.at[:, top, :], planes.at[:, before, :], 2, (lat, up))
    go_down = copy(planes.at[:, low, :], planes.at[:, after, :], 3, (lat, down))
    halo_up = copy(halo.at[:, top, :], halo.at[:, before, :], 4, (lat, up))
    halo_down = copy(halo.at[:, low, :], halo.at[:, after, :], 5, (lat, down))

    @pl.when(lat < nlat - 1)
    def _():
        go_right.start()

    @pl.when(lat > 0)
    def _():
        go_left.start()

    go_up.start()
    go_down.start()

    @pl.when(lat == 0)
    def _():
        halo[0, PAD:PAD + rows, :] = jnp.zeros((rows, lanes), jnp.float32)

    @pl.when(lat == nlat - 1)
    def _():
        halo[1, PAD:PAD + rows, :] = jnp.zeros((rows, lanes), jnp.float32)

    for k in range(work.shape[0]):
        for s in range(2):
            work[k, s, 0:PAD, :] = jnp.zeros((PAD, lanes), jnp.float32)
            work[k, s, ext + PAD:ext + 2 * PAD, :] = jnp.zeros((PAD, lanes), jnp.float32)

    @pl.when(lat > 0)
    def _():
        go_right.wait_recv()

    @pl.when(lat < nlat - 1)
    def _():
        go_left.wait_recv()

    halo_up.start()
    halo_down.start()
    go_up.wait()
    go_down.wait()
    halo_up.wait()
    halo_down.wait()

    @pl.when(lat < nlat - 1)
    def _():
        go_right.wait_send()

    @pl.when(lat > 0)
    def _():
        go_left.wait_send()

    chunks = [(a, min(CHUNK, ext - a)) for a in range(0, ext, CHUNK)]

    def unpack(p, a, n):
        left = pltpu.roll(halo[0, a:a + n, :], lax.rem(2 * lanes - EDGE - EDGE * p, lanes), 1)
        right = pltpu.roll(halo[1, a:a + n, :], lax.rem(2 * lanes - EDGE * p, lanes), 1)
        return jnp.where(lane < EDGE, right, jnp.where(lane >= lanes - EDGE, left, 0.0))

    for a, n in chunks:
        for s in range(2):
            if s:
                ocean, k = unpack(0, a, n), unpack(count, a, n)
            else:
                ocean, k = planes[0, a:a + n, :], planes[count, a:a + n, :]
            ocean = ocean * ocean
            coef[0, s, a:a + n, :] = ocean * (k + 0.25)
            coef[1, s, a:a + n, :] = 0.0625 * ocean

    at_first, at_last = lane == 0, lane == lanes - 1

    def apply(src, a, n, wide):
        o = a + PAD
        m, h = work[src, 0, o:o + n, :], work[src, 1, o:o + n, :]
        m_right, h_right = pltpu.roll(m, 1, 1), pltpu.roll(h, 1, 1)
        m_left, h_left = pltpu.roll(m, lanes - 1, 1), pltpu.roll(h, lanes - 1, 1)

        def one(s, x, a_side, b_side):
            total = work[src, s, o - 1:o + n - 1, :] + work[src, s, o + 1:o + n + 1, :]
            total = total + a_side + b_side
            return coef[0, s, a:a + n, :] * x - coef[1, s, a:a + n, :] * total

        out = one(0, m, jnp.where(at_first, h_right, m_right), jnp.where(at_last, h_left, m_left))
        if not wide:
            return out, None
        return out, one(
            1, h, jnp.where(at_first, m_right, h_right), jnp.where(at_last, m_left, h_left))

    def put(dst, a, n, pair):
        o = a + PAD
        work[dst, 0, o:o + n, :] = pair[0]
        work[dst, 1, o:o + n, :] = pair[1]

    def get(src, a, n):
        o = a + PAD
        return work[src, 0, o:o + n, :], work[src, 1, o:o + n, :]

    def probe(p, carry):
        for a, n in chunks:
            put(0, a, n, (planes[p, a:a + n, :], unpack(p, a, n)))
        for k in range(3):
            for a, n in chunks:
                put(k + 1, a, n, apply(k, a, n, True))
        for a, n in chunks:
            m, h = apply(3, a, n, True)
            m_old, h_old = get(2, a, n)
            put(4, a, n, (m - SHIFT * m_old, h - SHIFT * h_old))
        part = [jnp.zeros((8, lanes), jnp.float32) for _ in range(7)]
        step = 32
        for a in range(0, rows, step):
            w2, _ = apply(4, a + PAD, step, False)
            v0, w0, v1, w1, v2 = (get(k, a + PAD, step)[0] for k in range(5))
            k = kappa[a:a + step, :]
            kept[0, p, a:a + step, :] = v1
            kept[1, p, a:a + step, :] = v2
            for j, (v, w) in enumerate(((v0, w0), (v1, w1), (v2, w2))):
                at = pl.ds(pl.multiple_of((j * count + p) * rows + a, 8), step)
                terms[at, :] = k * (2.0 * v0 * w0) if j == 0 else k * (v * w0 + w * v0)
            pairs = ((w0, w0), (w0, w1), (w0, w2), (w1, w1), (w1, w2), (w2, w2), (v0, v0))
            for j, (x, y) in enumerate(pairs):
                xy = x * y
                for i in range(0, step, 8):
                    part[j] = part[j] + xy[i:i + 8]
        for j in range(7):
            dots[j, pl.ds(p, 1), :] = jnp.sum(part[j], axis=0, keepdims=True)
        return carry

    lax.fori_loop(0, count, probe, 0)

    def share(buf, mine, n, send, recv, axis):
        copies = []
        for d in range(1, n):
            other = lax.rem(mine + d, n)
            source = lax.rem(mine + n - d, n)
            device = (other, lon) if axis == 0 else (lat, other)
            pltpu.make_async_remote_copy(
                src_ref=buf.at[mine], dst_ref=buf.at[mine],
                send_sem=send.at[d - 1], recv_sem=recv.at[d - 1],
                device_id=device, device_id_type=MESH).start()
            copies.append(pltpu.make_async_remote_copy(
                src_ref=buf.at[mine], dst_ref=buf.at[source],
                send_sem=send.at[d - 1], recv_sem=recv.at[d - 1],
                device_id=device, device_id_type=MESH))
        return copies

    def gather(buf, n, copies):
        for c in copies:
            c.wait()
        total = buf[0]
        for i in range(1, n):
            total = total + buf[i]
        return total

    mine = jnp.zeros((count, lanes), jnp.float32)
    for j in range(7):
        mine = jnp.where(lane == j, jnp.sum(dots[j], axis=1, keepdims=True), mine)
    gram_lat[lat] = mine
    sent = share(gram_lat, lat, nlat, lat_send.at[0], lat_recv.at[0], 0)

    block = lax.broadcasted_iota(jnp.int32, (NB, lanes), 0)

    def sums(step, acc):
        lhs, rhs = [], []
        for i in range(2):
            z = step * 2 + i
            x = terms[pl.ds(z, 3 * count, stride=rows), :]
            high = x.astype(jnp.bfloat16)
            low = (x - high.astype(jnp.float32)).astype(jnp.bfloat16)
            lhs.append(jnp.concatenate([high, low], axis=0))
            hit = jnp.where(ids[pl.ds(z, 1), :] == block, 1.0, 0.0)
            rhs.append(hit.astype(jnp.bfloat16))
        return acc + lax.dot_general(
            jnp.concatenate(lhs, axis=1), jnp.concatenate(rhs, axis=1),
            (((1,), (1,)), ((), ())), preferred_element_type=jnp.float32)

    acc = jnp.zeros((6 * count, NB), jnp.float32)
    acc = lax.fori_loop(0, rows // 4, sums, acc, unroll=4)
    gram_lon[lon] = gather(gram_lat, nlat, sent)
    sent = share(gram_lon, lon, nlon, lon_send.at[0], lon_recv.at[0], 1)
    acc = lax.fori_loop(rows // 4, rows // 2, sums, acc, unroll=4)
    total = gather(gram_lon, nlon, sent)

    g = [total[:, j:j + 1] for j in range(7)]
    y = weights(tuple(g[:6]), (g[6], g[0], g[1] - SHIFT * g[0]))
    local = jnp.zeros((count, NB), jnp.float32)
    for j in range(3):
        ys[j] = jnp.broadcast_to(y[j], (count, lanes))
        at = j * count
        local = local + y[j] * (acc[at:at + count] + acc[at + 3 * count:at + 4 * count])
    sums_lat[lat] = jnp.concatenate([local, jnp.zeros_like(local)], axis=1)
    sent = share(sums_lat, lat, nlat, lat_send.at[1], lat_recv.at[1], 0)

    def finish(p, carry):
        y0, y1, y2 = (ys[j, pl.ds(p, 1), :] for j in range(3))
        solved[p] = y0 * planes[p, PAD:PAD + rows, :] + y1 * kept[0, p] + y2 * kept[1, p]
        t = [
            terms[pl.ds(pl.multiple_of((j * count + p) * rows, 8), rows), :] for j in range(3)]
        trace[p] = y0 * t[0] + y1 * t[1] + y2 * t[2]
        return carry

    lax.fori_loop(0, count // 2, finish, 0)
    sums_lon[lon] = gather(sums_lat, nlat, sent)
    sent = share(sums_lon, lon, nlon, lon_send.at[1], lon_recv.at[1], 1)
    lax.fori_loop(count // 2, count, finish, 0)
    total = gather(sums_lon, nlon, sent)
    traces[...] = total[:, :NB] * (NB / (rows * lanes * nlat * nlon))


def per_device(nlat, nlon, probe_signs, ocean_mask, kappa_sq, block_ids):
    count, rows, lanes = probe_signs.shape
    ext = rows + 2 * PAD
    f32 = jnp.float32
    vmem = pl.BlockSpec(memory_space=pltpu.VMEM)
    return pl.pallas_call(
        functools.partial(kernel, nlat, nlon),
        out_shape=(
            jax.ShapeDtypeStruct((count, rows, lanes), f32),
            jax.ShapeDtypeStruct((count, rows, lanes), f32),
            jax.ShapeDtypeStruct((count, NB), f32),
        ),
        in_specs=[vmem] * 4,
        out_specs=(vmem,) * 3,
        scratch_shapes=[
            pltpu.VMEM((count + 1, ext, lanes), f32),
            pltpu.VMEM((2, ext, lanes), f32),
            pltpu.VMEM((rows, lanes), f32),
            pltpu.VMEM((rows, lanes), f32),
            pltpu.VMEM((2, 2, ext, lanes), f32),
            pltpu.VMEM((5, 2, ext + 2 * PAD, lanes), f32),
            pltpu.VMEM((2, count, rows, lanes), f32),
            pltpu.VMEM((3 * count * rows, lanes), f32),
            pltpu.VMEM((8, count, lanes), f32),
            pltpu.VMEM((3, count, lanes), f32),
            pltpu.VMEM((nlat, count, lanes), f32),
            pltpu.VMEM((nlon, count, lanes), f32),
            pltpu.VMEM((nlat, count, lanes), f32),
            pltpu.VMEM((nlon, count, lanes), f32),
            pltpu.SemaphoreType.DMA((6,)),
            pltpu.SemaphoreType.DMA((6,)),
            pltpu.SemaphoreType.DMA((2, nlat - 1)),
            pltpu.SemaphoreType.DMA((2, nlat - 1)),
            pltpu.SemaphoreType.DMA((2, nlon - 1)),
            pltpu.SemaphoreType.DMA((2, nlon - 1)),
        ],
        compiler_params=pltpu.CompilerParams(
            collective_id=0, has_side_effects=True, vmem_limit_bytes=40 * 1024 * 1024),
    )(probe_signs, ocean_mask, kappa_sq, block_ids)


def solution(mesh):
    placed = (P(None, "lon", "lat"), P("lon", "lat"), P("lon", "lat"), P("lon", "lat"))
    return jax.shard_map(
        functools.partial(per_device, mesh.shape["lat"], mesh.shape["lon"]),
        mesh=mesh,
        in_specs=placed,
        out_specs=(P(None, "lon", "lat"), P(None, "lon", "lat"), P()),
        check_vma=False,
    )
```

```python
import functools

import jax
import jax.numpy as jnp
from jax import lax
from jax.experimental import pallas as pl
from jax.experimental.pallas import tpu as pltpu
from jax.sharding import PartitionSpec as P

NB = 64
EDGE = 7
PAD = 8
SHIFT = 0.4
FLOOR = 1e-6
CHUNK = 48
MESH = pl.DeviceIdType.MESH


def weights(gram, right):
    g00, g01, g02, g11, g12, g22 = gram
    r0, r1, r2 = right
    l10 = g01 / g00
    l20 = g02 / g00
    d1 = g11 - l10 * g01
    e12 = g12 - l10 * g02
    ok1 = d1 > FLOOR * g11
    i1 = jnp.where(ok1, 1.0 / jnp.where(ok1, d1, 1.0), 0.0)
    l21 = e12 * i1
    d2 = g22 - l20 * g02 - l21 * e12
    ok2 = d2 > FLOOR * g22
    i2 = jnp.where(ok2, 1.0 / jnp.where(ok2, d2, 1.0), 0.0)
    z1 = r1 - l10 * r0
    z2 = r2 - l20 * r0 - l21 * z1
    y2 = z2 * i2
    y1 = z1 * i1 - l21 * y2
    y0 = r0 / g00 - l10 * y1 - l20 * y2
    return y0, y1, y2


def kernel(
    nlat, nlon, signs_in, mask_in, kappa_in, ids_in, solved, trace, traces,
    signs, mask, kappa, ids, hits, planes, halo, left_edge, right_edge, coef, work, kept, terms, dots, ys,
    gram_lat, gram_lon, sums_lat, sums_lon,
    load_done, halo_send, halo_recv, lat_send, lat_recv, lon_send, lon_recv,
):
    loads = [
        pltpu.make_async_copy(src, dst, load_done.at[k])
        for k, (src, dst) in enumerate(
            ((signs_in, signs), (mask_in, mask), (kappa_in, kappa), (ids_in, ids)))]
    for load in loads:
        load.start()

    count, rows, lanes = signs.shape
    ext = rows + 2 * PAD
    lat, lon = lax.axis_index("lat"), lax.axis_index("lon")
    up, down = lax.rem(lon + 1, nlon), lax.rem(lon + nlon - 1, nlon)

    barrier = pltpu.get_barrier_semaphore()
    for d in range(1, nlat):
        pl.semaphore_signal(
            barrier, inc=1, device_id=(lax.rem(lat + d, nlat), lon), device_id_type=MESH)
    for d in range(1, nlon):
        pl.semaphore_signal(
            barrier, inc=1, device_id=(lat, lax.rem(lon + d, nlon)), device_id_type=MESH)
    has_left, has_right = lat > 0, lat < nlat - 1
    left, right = lax.max(lat - 1, 0), lax.min(lat + 1, nlat - 1)
    for there, side in ((has_left, left), (has_right, right)):
        @pl.when(there)
        def _(side=side):
            for end in (up, down):
                pl.semaphore_signal(
                    barrier, inc=1, device_id=(side, end), device_id_type=MESH)

    for load in loads[:3]:
        load.wait()
    lane = lax.broadcasted_iota(jnp.int32, (1, lanes), 1)

    def pack(step, carry):
        part = pl.ds(pl.multiple_of(step * 32, 32), 32)
        ocean = mask[part, :].astype(jnp.float32)
        first = jnp.zeros((32, lanes), jnp.float32)
        last = jnp.zeros((32, lanes), jnp.float32)
        for p in range(count + 1):
            if p < count:
                x = signs[p, part, :].astype(jnp.float32) * ocean
            else:
                x = kappa[part, :]
            planes[p, pl.ds(pl.multiple_of(step * 32 + PAD, 8), 32), :] = x
            here = (lane >= EDGE * p) & (lane < EDGE * (p + 1))
            first = jnp.where(here, pltpu.roll(x, EDGE * p, 1) if p else x, first)
            last = jnp.where(here, pltpu.roll(x, EDGE * (p + 1), 1), last)
        left_edge[part, :] = first
        right_edge[part, :] = last
        return carry

    lax.fori_loop(0, rows // 32, pack, 0)
    sides = lax.min(lat, 1) + lax.min(nlat - 1 - lat, 1)
    pl.semaphore_wait(barrier, nlat + nlon - 2 + 2 * sides)

    def copy(src, dst, k, device):
        return pltpu.make_async_remote_copy(
            src_ref=src, dst_ref=dst, send_sem=halo_send.at[k], recv_sem=halo_recv.at[k],
            device_id=device, device_id_type=MESH)

    own = pl.ds(PAD, rows)
    top, low = pl.ds(rows, PAD), pl.ds(PAD, PAD)
    before, after = pl.ds(0, PAD), pl.ds(rows + PAD, PAD)
    first_rows, last_rows = pl.ds(0, PAD), pl.ds(rows - PAD, PAD)
    go_right = [
        copy(right_edge, halo.at[0, own, :], 0, (right, lon)),
        copy(right_edge.at[last_rows, :], halo.at[0, before, :], 1, (right, up)),
        copy(right_edge.at[first_rows, :], halo.at[0, after, :], 2, (right, down)),
    ]
    go_left = [
        copy(left_edge, halo.at[1, own, :], 3, (left, lon)),
        copy(left_edge.at[last_rows, :], halo.at[1, before, :], 4, (left, up)),
        copy(left_edge.at[first_rows, :], halo.at[1, after, :], 5, (left, down)),
    ]
    go_lon = [
        copy(planes.at[:, top, :], planes.at[:, before, :], 6, (lat, up)),
        copy(planes.at[:, low, :], planes.at[:, after, :], 7, (lat, down)),
    ]

    @pl.when(has_right)
    def _():
        for c in go_right:
            c.start()

    @pl.when(has_left)
    def _():
        for c in go_left:
            c.start()

    for c in go_lon:
        c.start()

    @pl.when(lat == 0)
    def _():
        halo[0] = jnp.zeros((ext, lanes), jnp.float32)

    @pl.when(lat == nlat - 1)
    def _():
        halo[1] = jnp.zeros((ext, lanes), jnp.float32)

    for k in range(work.shape[0]):
        for s in range(2):
            work[k, s, 0:PAD, :] = jnp.zeros((PAD, lanes), jnp.float32)
            work[k, s, ext + PAD:ext + 2 * PAD, :] = jnp.zeros((PAD, lanes), jnp.float32)

    loads[3].wait()
    block = lax.broadcasted_iota(jnp.int32, (NB, lanes), 0)

    def mark(z, carry):
        hit = jnp.where(ids[pl.ds(z, 1), :] == block, 1.0, 0.0)
        hits[pl.ds(pl.multiple_of(z * NB, NB), NB), :] = hit.astype(jnp.bfloat16)
        return carry

    lax.fori_loop(0, rows, mark, 0, unroll=4)

    for c in go_lon:
        c.wait()

    @pl.when(has_left)
    def _():
        for c in go_right:
            c.wait_recv()
        for c in go_left:
            c.wait_send()

    @pl.when(has_right)
    def _():
        for c in go_left:
            c.wait_recv()
        for c in go_right:
            c.wait_send()

    chunks = [(a, min(CHUNK, ext - a)) for a in range(0, ext, CHUNK)]

    def unpack(p, a, n):
        left = pltpu.roll(halo[0, a:a + n, :], lax.rem(2 * lanes - EDGE - EDGE * p, lanes), 1)
        right = pltpu.roll(halo[1, a:a + n, :], lax.rem(2 * lanes - EDGE * p, lanes), 1)
        return jnp.where(lane < EDGE, right, jnp.where(lane >= lanes - EDGE, left, 0.0))

    for a, n in chunks:
        for s in range(2):
            if s:
                ocean, k = unpack(0, a, n), unpack(count, a, n)
            else:
                ocean, k = planes[0, a:a + n, :], planes[count, a:a + n, :]
            ocean = ocean * ocean
            coef[0, s, a:a + n, :] = ocean * (k + 0.25)
            coef[1, s, a:a + n, :] = 0.0625 * ocean

    at_first, at_last = lane == 0, lane == lanes - 1

    def apply(src, a, n, wide):
        o = a + PAD
        m, h = work[src, 0, o:o + n, :], work[src, 1, o:o + n, :]
        m_right, h_right = pltpu.roll(m, 1, 1), pltpu.roll(h, 1, 1)
        m_left, h_left = pltpu.roll(m, lanes - 1, 1), pltpu.roll(h, lanes - 1, 1)

        def one(s, x, a_side, b_side):
            total = work[src, s, o - 1:o + n - 1, :] + work[src, s, o + 1:o + n + 1, :]
            total = total + a_side + b_side
            return coef[0, s, a:a + n, :] * x - coef[1, s, a:a + n, :] * total

        out = one(0, m, jnp.where(at_first, h_right, m_right), jnp.where(at_last, h_left, m_left))
        if not wide:
            return out, None
        return out, one(
            1, h, jnp.where(at_first, m_right, h_right), jnp.where(at_last, m_left, h_left))

    def put(dst, a, n, pair):
        o = a + PAD
        work[dst, 0, o:o + n, :] = pair[0]
        work[dst, 1, o:o + n, :] = pair[1]

    def get(src, a, n):
        o = a + PAD
        return work[src, 0, o:o + n, :], work[src, 1, o:o + n, :]

    def probe(p, carry):
        for a, n in chunks:
            put(0, a, n, (planes[p, a:a + n, :], unpack(p, a, n)))
        for k in range(3):
            for a, n in chunks:
                put(k + 1, a, n, apply(k, a, n, True))
        for a, n in chunks:
            m, h = apply(3, a, n, True)
            m_old, h_old = get(2, a, n)
            put(4, a, n, (m - SHIFT * m_old, h - SHIFT * h_old))
        part = [jnp.zeros((8, lanes), jnp.float32) for _ in range(7)]
        step = 32
        for a in range(0, rows, step):
            w2, _ = apply(4, a + PAD, step, False)
            v0, w0, v1, w1, v2 = (get(k, a + PAD, step)[0] for k in range(5))
            k = kappa[a:a + step, :]
            kept[0, p, a:a + step, :] = v1
            kept[1, p, a:a + step, :] = v2
            for j, (v, w) in enumerate(((v0, w0), (v1, w1), (v2, w2))):
                at = pl.ds(pl.multiple_of((j * count + p) * rows + a, 8), step)
                terms[at, :] = k * (2.0 * v0 * w0) if j == 0 else k * (v * w0 + w * v0)
            pairs = ((w0, w0), (w0, w1), (w0, w2), (w1, w1), (w1, w2), (w2, w2), (v0, v0))
            for j, (x, y) in enumerate(pairs):
                xy = x * y
                for i in range(0, step, 8):
                    part[j] = part[j] + xy[i:i + 8]
        for j in range(7):
            dots[j, pl.ds(p, 1), :] = jnp.sum(part[j], axis=0, keepdims=True)
        return carry

    lax.fori_loop(0, count, probe, 0)

    def share(buf, mine, n, send, recv, axis):
        copies = []
        for d in range(1, n):
            other = lax.rem(mine + d, n)
            source = lax.rem(mine + n - d, n)
            device = (other, lon) if axis == 0 else (lat, other)
            pltpu.make_async_remote_copy(
                src_ref=buf.at[mine], dst_ref=buf.at[mine],
                send_sem=send.at[d - 1], recv_sem=recv.at[d - 1],
                device_id=device, device_id_type=MESH).start()
            copies.append(pltpu.make_async_remote_copy(
                src_ref=buf.at[mine], dst_ref=buf.at[source],
                send_sem=send.at[d - 1], recv_sem=recv.at[d - 1],
                device_id=device, device_id_type=MESH))
        return copies

    def gather(buf, n, copies):
        for c in copies:
            c.wait()
        total = buf[0]
        for i in range(1, n):
            total = total + buf[i]
        return total

    mine = jnp.zeros((count, lanes), jnp.float32)
    for j in range(7):
        mine = jnp.where(lane == j, jnp.sum(dots[j], axis=1, keepdims=True), mine)
    gram_lat[lat] = mine
    sent = share(gram_lat, lat, nlat, lat_send.at[0], lat_recv.at[0], 0)

    def sums(step, acc):
        lhs, rhs = [], []
        for i in range(2):
            z = step * 2 + i
            x = terms[pl.ds(z, 3 * count, stride=rows), :]
            high = x.astype(jnp.bfloat16)
            low = (x - high.astype(jnp.float32)).astype(jnp.bfloat16)
            lhs.append(jnp.concatenate([high, low], axis=0))
            rhs.append(hits[pl.ds(pl.multiple_of(z * NB, NB), NB), :])
        return acc + lax.dot_general(
            jnp.concatenate(lhs, axis=1), jnp.concatenate(rhs, axis=1),
            (((1,), (1,)), ((), ())), preferred_element_type=jnp.float32)

    acc = jnp.zeros((6 * count, NB), jnp.float32)
    acc = lax.fori_loop(0, rows // 4, sums, acc, unroll=4)
    gram_lon[lon] = gather(gram_lat, nlat, sent)
    sent = share(gram_lon, lon, nlon, lon_send.at[0], lon_recv.at[0], 1)
    acc = lax.fori_loop(rows // 4, rows // 2, sums, acc, unroll=4)
    half = 3 * count // 2
    acc = acc[:3 * count] + acc[3 * count:]
    sums_lat[lat] = jnp.concatenate([acc[:half], acc[half:]], axis=1)
    sums_sent = share(sums_lat, lat, nlat, lat_send.at[1], lat_recv.at[1], 0)
    total = gather(gram_lon, nlon, sent)

    g = [total[:, j:j + 1] for j in range(7)]
    y = weights(tuple(g[:6]), (g[6], g[0], g[1] - SHIFT * g[0]))
    for j in range(3):
        ys[j] = jnp.broadcast_to(y[j], (count, lanes))
    acc = gather(sums_lat, nlat, sums_sent)
    acc = jnp.concatenate([acc[:, :NB], acc[:, NB:]], axis=0)
    local = y[0] * acc[:count] + y[1] * acc[count:2 * count] + y[2] * acc[2 * count:]
    sums_lon[lon] = jnp.concatenate([local[:count // 2], local[count // 2:]], axis=1)
    sent = share(sums_lon, lon, nlon, lon_send.at[1], lon_recv.at[1], 1)

    def finish(p, carry):
        y0, y1, y2 = (ys[j, pl.ds(p, 1), :] for j in range(3))
        solved[p] = y0 * planes[p, PAD:PAD + rows, :] + y1 * kept[0, p] + y2 * kept[1, p]
        t = [
            terms[pl.ds(pl.multiple_of((j * count + p) * rows, 8), rows), :] for j in range(3)]
        trace[p] = y0 * t[0] + y1 * t[1] + y2 * t[2]
        return carry

    lax.fori_loop(0, count, finish, 0)
    total = gather(sums_lon, nlon, sent)
    total = jnp.concatenate([total[:, :NB], total[:, NB:]], axis=0)
    traces[...] = total / jnp.float32(rows * lanes * nlat * nlon // NB)


def per_device(nlat, nlon, probe_signs, ocean_mask, kappa_sq, block_ids):
    count, rows, lanes = probe_signs.shape
    ext = rows + 2 * PAD
    f32 = jnp.float32
    vmem = pl.BlockSpec(memory_space=pltpu.VMEM)
    return pl.pallas_call(
        functools.partial(kernel, nlat, nlon),
        out_shape=(
            jax.ShapeDtypeStruct((count, rows, lanes), f32),
            jax.ShapeDtypeStruct((count, rows, lanes), f32),
            jax.ShapeDtypeStruct((count, NB), f32),
        ),
        in_specs=[pl.BlockSpec(memory_space=pltpu.HBM)] * 4,
        out_specs=(vmem,) * 3,
        scratch_shapes=[
            pltpu.VMEM((count, rows, lanes), jnp.int32),
            pltpu.VMEM((rows, lanes), jnp.int32),
            pltpu.VMEM((rows, lanes), f32),
            pltpu.VMEM((rows, lanes), jnp.int32),
            pltpu.VMEM((rows * NB, lanes), jnp.bfloat16),
            pltpu.VMEM((count + 1, ext, lanes), f32),
            pltpu.VMEM((2, ext, lanes), f32),
            pltpu.VMEM((rows, lanes), f32),
            pltpu.VMEM((rows, lanes), f32),
            pltpu.VMEM((2, 2, ext, lanes), f32),
            pltpu.VMEM((5, 2, ext + 2 * PAD, lanes), f32),
            pltpu.VMEM((2, count, rows, lanes), f32),
            pltpu.VMEM((3 * count * rows, lanes), f32),
            pltpu.VMEM((8, count, lanes), f32),
            pltpu.VMEM((3, count, lanes), f32),
            pltpu.VMEM((nlat, count, lanes), f32),
            pltpu.VMEM((nlon, count, lanes), f32),
            pltpu.VMEM((nlat, 3 * count // 2, lanes), f32),
            pltpu.VMEM((nlon, count // 2, lanes), f32),
            pltpu.SemaphoreType.DMA((4,)),
            pltpu.SemaphoreType.DMA((8,)),
            pltpu.SemaphoreType.DMA((8,)),
            pltpu.SemaphoreType.DMA((2, nlat - 1)),
            pltpu.SemaphoreType.DMA((2, nlat - 1)),
            pltpu.SemaphoreType.DMA((2, nlon - 1)),
            pltpu.SemaphoreType.DMA((2, nlon - 1)),
        ],
        compiler_params=pltpu.CompilerParams(
            collective_id=0, has_side_effects=True, vmem_limit_bytes=40 * 1024 * 1024),
    )(probe_signs, ocean_mask, kappa_sq, block_ids)


def solution(mesh):
    placed = (P(None, "lon", "lat"), P("lon", "lat"), P("lon", "lat"), P("lon", "lat"))
    return jax.shard_map(
        functools.partial(per_device, mesh.shape["lat"], mesh.shape["lon"]),
        mesh=mesh,
        in_specs=placed,
        out_specs=(P(None, "lon", "lat"), P(None, "lon", "lat"), P()),
        check_vma=False,
    )
```

```python
import functools

import jax
import jax.numpy as jnp
from jax import lax
from jax.experimental import pallas as pl
from jax.experimental.pallas import tpu as pltpu
from jax.sharding import PartitionSpec as P

NB = 64
EDGE = 7
PAD = 8
SHIFT = 0.4
FLOOR = 1e-6
CHUNK = 48
MESH = pl.DeviceIdType.MESH


def weights(gram, right):
    g00, g01, g02, g11, g12, g22 = gram
    r0, r1, r2 = right
    l10 = g01 / g00
    l20 = g02 / g00
    d1 = g11 - l10 * g01
    e12 = g12 - l10 * g02
    ok1 = d1 > FLOOR * g11
    i1 = jnp.where(ok1, 1.0 / jnp.where(ok1, d1, 1.0), 0.0)
    l21 = e12 * i1
    d2 = g22 - l20 * g02 - l21 * e12
    ok2 = d2 > FLOOR * g22
    i2 = jnp.where(ok2, 1.0 / jnp.where(ok2, d2, 1.0), 0.0)
    z1 = r1 - l10 * r0
    z2 = r2 - l20 * r0 - l21 * z1
    y2 = z2 * i2
    y1 = z1 * i1 - l21 * y2
    y0 = r0 / g00 - l10 * y1 - l20 * y2
    return y0, y1, y2


def kernel(
    nlat, nlon, signs_in, mask_in, kappa_in, ids_in, solved_out, trace_out, traces,
    solved, trace, signs, mask, kappa, ids, hits, planes, halo, left_edge, right_edge, coef, work, kept, terms, dots, ys,
    gram_lat, gram_lon, sums_lat, sums_lon,
    load_done, store_done, halo_send, halo_recv, lat_send, lat_recv, lon_send, lon_recv,
):
    loads = [
        pltpu.make_async_copy(src, dst, load_done.at[k])
        for k, (src, dst) in enumerate(
            ((signs_in, signs), (mask_in, mask), (kappa_in, kappa), (ids_in, ids)))]
    for load in loads:
        load.start()

    count, rows, lanes = signs.shape
    ext = rows + 2 * PAD
    lat, lon = lax.axis_index("lat"), lax.axis_index("lon")
    up, down = lax.rem(lon + 1, nlon), lax.rem(lon + nlon - 1, nlon)

    barrier = pltpu.get_barrier_semaphore()
    for d in range(1, nlat):
        pl.semaphore_signal(
            barrier, inc=1, device_id=(lax.rem(lat + d, nlat), lon), device_id_type=MESH)
    for d in range(1, nlon):
        pl.semaphore_signal(
            barrier, inc=1, device_id=(lat, lax.rem(lon + d, nlon)), device_id_type=MESH)
    has_left, has_right = lat > 0, lat < nlat - 1
    left, right = lax.max(lat - 1, 0), lax.min(lat + 1, nlat - 1)
    for there, side in ((has_left, left), (has_right, right)):
        @pl.when(there)
        def _(side=side):
            for end in (up, down):
                pl.semaphore_signal(
                    barrier, inc=1, device_id=(side, end), device_id_type=MESH)

    for load in loads[:3]:
        load.wait()
    lane = lax.broadcasted_iota(jnp.int32, (1, lanes), 1)

    def pack(step, carry):
        part = pl.ds(pl.multiple_of(step * 32, 32), 32)
        ocean = mask[part, :].astype(jnp.float32)
        first = jnp.zeros((32, lanes), jnp.float32)
        last = jnp.zeros((32, lanes), jnp.float32)
        for p in range(count + 1):
            if p < count:
                x = signs[p, part, :].astype(jnp.float32) * ocean
            else:
                x = kappa[part, :]
            planes[p, pl.ds(pl.multiple_of(step * 32 + PAD, 8), 32), :] = x
            here = (lane >= EDGE * p) & (lane < EDGE * (p + 1))
            first = jnp.where(here, pltpu.roll(x, EDGE * p, 1) if p else x, first)
            last = jnp.where(here, pltpu.roll(x, EDGE * (p + 1), 1), last)
        left_edge[part, :] = first
        right_edge[part, :] = last
        return carry

    lax.fori_loop(0, rows // 32, pack, 0)
    sides = lax.min(lat, 1) + lax.min(nlat - 1 - lat, 1)
    pl.semaphore_wait(barrier, nlat + nlon - 2 + 2 * sides)

    def copy(src, dst, k, device):
        return pltpu.make_async_remote_copy(
            src_ref=src, dst_ref=dst, send_sem=halo_send.at[k], recv_sem=halo_recv.at[k],
            device_id=device, device_id_type=MESH)

    own = pl.ds(PAD, rows)
    top, low = pl.ds(rows, PAD), pl.ds(PAD, PAD)
    before, after = pl.ds(0, PAD), pl.ds(rows + PAD, PAD)
    first_rows, last_rows = pl.ds(0, PAD), pl.ds(rows - PAD, PAD)
    go_right = [
        copy(right_edge, halo.at[0, own, :], 0, (right, lon)),
        copy(right_edge.at[last_rows, :], halo.at[0, before, :], 1, (right, up)),
        copy(right_edge.at[first_rows, :], halo.at[0, after, :], 2, (right, down)),
    ]
    go_left = [
        copy(left_edge, halo.at[1, own, :], 3, (left, lon)),
        copy(left_edge.at[last_rows, :], halo.at[1, before, :], 4, (left, up)),
        copy(left_edge.at[first_rows, :], halo.at[1, after, :], 5, (left, down)),
    ]
    go_lon = [
        copy(planes.at[:, top, :], planes.at[:, before, :], 6, (lat, up)),
        copy(planes.at[:, low, :], planes.at[:, after, :], 7, (lat, down)),
    ]

    @pl.when(has_right)
    def _():
        for c in go_right:
            c.start()

    @pl.when(has_left)
    def _():
        for c in go_left:
            c.start()

    for c in go_lon:
        c.start()

    @pl.when(lat == 0)
    def _():
        halo[0] = jnp.zeros((ext, lanes), jnp.float32)

    @pl.when(lat == nlat - 1)
    def _():
        halo[1] = jnp.zeros((ext, lanes), jnp.float32)

    for k in range(work.shape[0]):
        for s in range(2):
            work[k, s, 0:PAD, :] = jnp.zeros((PAD, lanes), jnp.float32)
            work[k, s, ext + PAD:ext + 2 * PAD, :] = jnp.zeros((PAD, lanes), jnp.float32)

    loads[3].wait()
    block = lax.broadcasted_iota(jnp.int32, (NB, lanes), 0)

    def mark(z, carry):
        hit = jnp.where(ids[pl.ds(z, 1), :] == block, 1.0, 0.0)
        hits[pl.ds(pl.multiple_of(z * NB, NB), NB), :] = hit.astype(jnp.bfloat16)
        return carry

    lax.fori_loop(0, rows, mark, 0, unroll=4)

    for c in go_lon:
        c.wait()

    @pl.when(has_left)
    def _():
        for c in go_right:
            c.wait_recv()
        for c in go_left:
            c.wait_send()

    @pl.when(has_right)
    def _():
        for c in go_left:
            c.wait_recv()
        for c in go_right:
            c.wait_send()

    chunks = [(a, min(CHUNK, ext - a)) for a in range(0, ext, CHUNK)]

    def unpack(p, a, n):
        left = pltpu.roll(halo[0, a:a + n, :], lax.rem(2 * lanes - EDGE - EDGE * p, lanes), 1)
        right = pltpu.roll(halo[1, a:a + n, :], lax.rem(2 * lanes - EDGE * p, lanes), 1)
        return jnp.where(lane < EDGE, right, jnp.where(lane >= lanes - EDGE, left, 0.0))

    for a, n in chunks:
        for s in range(2):
            if s:
                ocean, k = unpack(0, a, n), unpack(count, a, n)
            else:
                ocean, k = planes[0, a:a + n, :], planes[count, a:a + n, :]
            ocean = ocean * ocean
            coef[0, s, a:a + n, :] = ocean * (k + 0.25)
            coef[1, s, a:a + n, :] = 0.0625 * ocean

    at_first, at_last = lane == 0, lane == lanes - 1

    def apply(src, a, n, wide):
        o = a + PAD
        m, h = work[src, 0, o:o + n, :], work[src, 1, o:o + n, :]
        m_right, h_right = pltpu.roll(m, 1, 1), pltpu.roll(h, 1, 1)
        m_left, h_left = pltpu.roll(m, lanes - 1, 1), pltpu.roll(h, lanes - 1, 1)

        def one(s, x, a_side, b_side):
            total = work[src, s, o - 1:o + n - 1, :] + work[src, s, o + 1:o + n + 1, :]
            total = total + a_side + b_side
            return coef[0, s, a:a + n, :] * x - coef[1, s, a:a + n, :] * total

        out = one(0, m, jnp.where(at_first, h_right, m_right), jnp.where(at_last, h_left, m_left))
        if not wide:
            return out, None
        return out, one(
            1, h, jnp.where(at_first, m_right, h_right), jnp.where(at_last, m_left, h_left))

    def put(dst, a, n, pair):
        o = a + PAD
        work[dst, 0, o:o + n, :] = pair[0]
        work[dst, 1, o:o + n, :] = pair[1]

    def get(src, a, n):
        o = a + PAD
        return work[src, 0, o:o + n, :], work[src, 1, o:o + n, :]

    def probe(p, carry):
        for a, n in chunks:
            put(0, a, n, (planes[p, a:a + n, :], unpack(p, a, n)))
        for k in range(3):
            for a, n in chunks:
                put(k + 1, a, n, apply(k, a, n, True))
        for a, n in chunks:
            m, h = apply(3, a, n, True)
            m_old, h_old = get(2, a, n)
            put(4, a, n, (m - SHIFT * m_old, h - SHIFT * h_old))
        part = [jnp.zeros((8, lanes), jnp.float32) for _ in range(7)]
        step = 32
        for a in range(0, rows, step):
            w2, _ = apply(4, a + PAD, step, False)
            v0, w0, v1, w1, v2 = (get(k, a + PAD, step)[0] for k in range(5))
            k = kappa[a:a + step, :]
            kept[0, p, a:a + step, :] = v1
            kept[1, p, a:a + step, :] = v2
            for j, (v, w) in enumerate(((v0, w0), (v1, w1), (v2, w2))):
                at = pl.ds(pl.multiple_of((j * count + p) * rows + a, 8), step)
                terms[at, :] = k * (2.0 * v0 * w0) if j == 0 else k * (v * w0 + w * v0)
            pairs = ((w0, w0), (w0, w1), (w0, w2), (w1, w1), (w1, w2), (w2, w2), (v0, v0))
            for j, (x, y) in enumerate(pairs):
                xy = x * y
                for i in range(0, step, 8):
                    part[j] = part[j] + xy[i:i + 8]
        for j in range(7):
            dots[j, pl.ds(p, 1), :] = jnp.sum(part[j], axis=0, keepdims=True)
        return carry

    lax.fori_loop(0, count, probe, 0)

    def share(buf, mine, n, send, recv, axis):
        copies = []
        for d in range(1, n):
            other = lax.rem(mine + d, n)
            source = lax.rem(mine + n - d, n)
            device = (other, lon) if axis == 0 else (lat, other)
            pltpu.make_async_remote_copy(
                src_ref=buf.at[mine], dst_ref=buf.at[mine],
                send_sem=send.at[d - 1], recv_sem=recv.at[d - 1],
                device_id=device, device_id_type=MESH).start()
            copies.append(pltpu.make_async_remote_copy(
                src_ref=buf.at[mine], dst_ref=buf.at[source],
                send_sem=send.at[d - 1], recv_sem=recv.at[d - 1],
                device_id=device, device_id_type=MESH))
        return copies

    def gather(buf, n, copies):
        for c in copies:
            c.wait()
        total = buf[0]
        for i in range(1, n):
            total = total + buf[i]
        return total

    mine = jnp.zeros((count, lanes), jnp.float32)
    for j in range(7):
        mine = jnp.where(lane == j, jnp.sum(dots[j], axis=1, keepdims=True), mine)
    gram_lat[lat] = mine
    sent = share(gram_lat, lat, nlat, lat_send.at[0], lat_recv.at[0], 0)

    def sums(step, acc):
        lhs, rhs = [], []
        for i in range(2):
            z = step * 2 + i
            x = terms[pl.ds(z, 3 * count, stride=rows), :]
            high = x.astype(jnp.bfloat16)
            low = (x - high.astype(jnp.float32)).astype(jnp.bfloat16)
            lhs.append(jnp.concatenate([high, low], axis=0))
            rhs.append(hits[pl.ds(pl.multiple_of(z * NB, NB), NB), :])
        return acc + lax.dot_general(
            jnp.concatenate(lhs, axis=1), jnp.concatenate(rhs, axis=1),
            (((1,), (1,)), ((), ())), preferred_element_type=jnp.float32)

    acc = jnp.zeros((6 * count, NB), jnp.float32)
    acc = lax.fori_loop(0, rows // 4, sums, acc, unroll=4)
    gram_lon[lon] = gather(gram_lat, nlat, sent)
    sent = share(gram_lon, lon, nlon, lon_send.at[0], lon_recv.at[0], 1)
    acc = lax.fori_loop(rows // 4, rows // 2, sums, acc, unroll=4)
    half = 3 * count // 2
    acc = acc[:3 * count] + acc[3 * count:]
    sums_lat[lat] = jnp.concatenate([acc[:half], acc[half:]], axis=1)
    sums_sent = share(sums_lat, lat, nlat, lat_send.at[1], lat_recv.at[1], 0)
    total = gather(gram_lon, nlon, sent)

    g = [total[:, j:j + 1] for j in range(7)]
    y = weights(tuple(g[:6]), (g[6], g[0], g[1] - SHIFT * g[0]))
    for j in range(3):
        ys[j] = jnp.broadcast_to(y[j], (count, lanes))
    acc = gather(sums_lat, nlat, sums_sent)
    acc = jnp.concatenate([acc[:, :NB], acc[:, NB:]], axis=0)
    local = y[0] * acc[:count] + y[1] * acc[count:2 * count] + y[2] * acc[2 * count:]
    sums_lon[lon] = jnp.concatenate([local[:count // 2], local[count // 2:]], axis=1)
    sent = share(sums_lon, lon, nlon, lon_send.at[1], lon_recv.at[1], 1)

    def finish(p, carry):
        y0, y1, y2 = (ys[j, pl.ds(p, 1), :] for j in range(3))
        solved[p] = y0 * planes[p, PAD:PAD + rows, :] + y1 * kept[0, p] + y2 * kept[1, p]
        t = [
            terms[pl.ds(pl.multiple_of((j * count + p) * rows, 8), rows), :] for j in range(3)]
        trace[p] = y0 * t[0] + y1 * t[1] + y2 * t[2]
        return carry

    stores = []
    part = count // 4
    for k in range(4):
        lax.fori_loop(k * part, (k + 1) * part, finish, 0)
        at = pl.ds(k * part, part)
        for j, (src, dst) in enumerate(((solved, solved_out), (trace, trace_out))):
            stores.append(pltpu.make_async_copy(src.at[at], dst.at[at], store_done.at[k, j]))
            stores[-1].start()
    total = gather(sums_lon, nlon, sent)
    total = jnp.concatenate([total[:, :NB], total[:, NB:]], axis=0)
    traces[...] = total / jnp.float32(rows * lanes * nlat * nlon // NB)
    for store in stores:
        store.wait()


def per_device(nlat, nlon, probe_signs, ocean_mask, kappa_sq, block_ids):
    count, rows, lanes = probe_signs.shape
    ext = rows + 2 * PAD
    f32 = jnp.float32
    vmem = pl.BlockSpec(memory_space=pltpu.VMEM)
    return pl.pallas_call(
        functools.partial(kernel, nlat, nlon),
        out_shape=(
            jax.ShapeDtypeStruct((count, rows, lanes), f32),
            jax.ShapeDtypeStruct((count, rows, lanes), f32),
            jax.ShapeDtypeStruct((count, NB), f32),
        ),
        in_specs=[pl.BlockSpec(memory_space=pltpu.HBM)] * 4,
        out_specs=(pl.BlockSpec(memory_space=pltpu.HBM),) * 2 + (vmem,),
        scratch_shapes=[
            pltpu.VMEM((count, rows, lanes), f32),
            pltpu.VMEM((count, rows, lanes), f32),
            pltpu.VMEM((count, rows, lanes), jnp.int32),
            pltpu.VMEM((rows, lanes), jnp.int32),
            pltpu.VMEM((rows, lanes), f32),
            pltpu.VMEM((rows, lanes), jnp.int32),
            pltpu.VMEM((rows * NB, lanes), jnp.bfloat16),
            pltpu.VMEM((count + 1, ext, lanes), f32),
            pltpu.VMEM((2, ext, lanes), f32),
            pltpu.VMEM((rows, lanes), f32),
            pltpu.VMEM((rows, lanes), f32),
            pltpu.VMEM((2, 2, ext, lanes), f32),
            pltpu.VMEM((5, 2, ext + 2 * PAD, lanes), f32),
            pltpu.VMEM((2, count, rows, lanes), f32),
            pltpu.VMEM((3 * count * rows, lanes), f32),
            pltpu.VMEM((8, count, lanes), f32),
            pltpu.VMEM((3, count, lanes), f32),
            pltpu.VMEM((nlat, count, lanes), f32),
            pltpu.VMEM((nlon, count, lanes), f32),
            pltpu.VMEM((nlat, 3 * count // 2, lanes), f32),
            pltpu.VMEM((nlon, count // 2, lanes), f32),
            pltpu.SemaphoreType.DMA((4,)),
            pltpu.SemaphoreType.DMA((4, 2)),
            pltpu.SemaphoreType.DMA((8,)),
            pltpu.SemaphoreType.DMA((8,)),
            pltpu.SemaphoreType.DMA((2, nlat - 1)),
            pltpu.SemaphoreType.DMA((2, nlat - 1)),
            pltpu.SemaphoreType.DMA((2, nlon - 1)),
            pltpu.SemaphoreType.DMA((2, nlon - 1)),
        ],
        compiler_params=pltpu.CompilerParams(
            collective_id=0, has_side_effects=True, vmem_limit_bytes=64 * 1024 * 1024),
    )(probe_signs, ocean_mask, kappa_sq, block_ids)


def solution(mesh):
    placed = (P(None, "lon", "lat"), P("lon", "lat"), P("lon", "lat"), P("lon", "lat"))
    return jax.shard_map(
        functools.partial(per_device, mesh.shape["lat"], mesh.shape["lon"]),
        mesh=mesh,
        in_specs=placed,
        out_specs=(P(None, "lon", "lat"), P(None, "lon", "lat"), P()),
        check_vma=False,
    )
```

```python
import functools

import jax
import jax.numpy as jnp
from jax import lax
from jax.experimental import pallas as pl
from jax.experimental.pallas import tpu as pltpu
from jax.sharding import PartitionSpec as P

NB = 64
EDGE = 7
PAD = 8
SHIFT = 0.4
FLOOR = 1e-6
CHUNK = 48
GROUP = 4
MESH = pl.DeviceIdType.MESH


def weights(gram, right):
    g00, g01, g02, g11, g12, g22 = gram
    r0, r1, r2 = right
    l10 = g01 / g00
    l20 = g02 / g00
    d1 = g11 - l10 * g01
    e12 = g12 - l10 * g02
    ok1 = d1 > FLOOR * g11
    i1 = jnp.where(ok1, 1.0 / jnp.where(ok1, d1, 1.0), 0.0)
    l21 = e12 * i1
    d2 = g22 - l20 * g02 - l21 * e12
    ok2 = d2 > FLOOR * g22
    i2 = jnp.where(ok2, 1.0 / jnp.where(ok2, d2, 1.0), 0.0)
    z1 = r1 - l10 * r0
    z2 = r2 - l20 * r0 - l21 * z1
    y2 = z2 * i2
    y1 = z1 * i1 - l21 * y2
    y0 = r0 / g00 - l10 * y1 - l20 * y2
    return y0, y1, y2


def kernel(
    nlat, nlon, signs_in, mask_in, kappa_in, ids_in, solved_out, trace_out, traces,
    solved, trace, signs, mask, kappa, ids, hits, planes, halo, left_edge, right_edge, coef, work, kept, terms, dots, ys,
    gram_lat, gram_lon, sums_lat, sums_lon,
    load_done, store_done, halo_send, halo_recv, lat_send, lat_recv, lon_send, lon_recv,
):
    loads = [
        pltpu.make_async_copy(src, dst, load_done.at[k])
        for k, (src, dst) in enumerate(
            ((signs_in, signs), (mask_in, mask), (kappa_in, kappa), (ids_in, ids)))]
    for load in loads:
        load.start()

    count, rows, lanes = signs.shape
    ext = rows + 2 * PAD
    lat, lon = lax.axis_index("lat"), lax.axis_index("lon")
    up, down = lax.rem(lon + 1, nlon), lax.rem(lon + nlon - 1, nlon)

    barrier = pltpu.get_barrier_semaphore()
    for d in range(1, nlat):
        pl.semaphore_signal(
            barrier, inc=1, device_id=(lax.rem(lat + d, nlat), lon), device_id_type=MESH)
    for d in range(1, nlon):
        pl.semaphore_signal(
            barrier, inc=1, device_id=(lat, lax.rem(lon + d, nlon)), device_id_type=MESH)
    has_left, has_right = lat > 0, lat < nlat - 1
    left, right = lax.max(lat - 1, 0), lax.min(lat + 1, nlat - 1)
    for there, side in ((has_left, left), (has_right, right)):
        @pl.when(there)
        def _(side=side):
            for end in (up, down):
                pl.semaphore_signal(
                    barrier, inc=1, device_id=(side, end), device_id_type=MESH)

    for load in loads[:3]:
        load.wait()
    lane = lax.broadcasted_iota(jnp.int32, (1, lanes), 1)

    def pack(step, carry):
        part = pl.ds(pl.multiple_of(step * 32, 32), 32)
        ocean = mask[part, :].astype(jnp.float32)
        first = jnp.zeros((32, lanes), jnp.float32)
        last = jnp.zeros((32, lanes), jnp.float32)
        for p in range(count + 1):
            if p < count:
                x = signs[p, part, :].astype(jnp.float32) * ocean
            else:
                x = kappa[part, :]
            planes[p, pl.ds(pl.multiple_of(step * 32 + PAD, 8), 32), :] = x
            here = (lane >= EDGE * p) & (lane < EDGE * (p + 1))
            first = jnp.where(here, pltpu.roll(x, EDGE * p, 1) if p else x, first)
            last = jnp.where(here, pltpu.roll(x, EDGE * (p + 1), 1), last)
        left_edge[part, :] = first
        right_edge[part, :] = last
        return carry

    lax.fori_loop(0, rows // 32, pack, 0)
    sides = lax.min(lat, 1) + lax.min(nlat - 1 - lat, 1)
    pl.semaphore_wait(barrier, nlat + nlon - 2 + 2 * sides)

    def copy(src, dst, k, device):
        return pltpu.make_async_remote_copy(
            src_ref=src, dst_ref=dst, send_sem=halo_send.at[k], recv_sem=halo_recv.at[k],
            device_id=device, device_id_type=MESH)

    own = pl.ds(PAD, rows)
    top, low = pl.ds(rows, PAD), pl.ds(PAD, PAD)
    before, after = pl.ds(0, PAD), pl.ds(rows + PAD, PAD)
    first_rows, last_rows = pl.ds(0, PAD), pl.ds(rows - PAD, PAD)
    go_right = [
        copy(right_edge, halo.at[0, own, :], 0, (right, lon)),
        copy(right_edge.at[last_rows, :], halo.at[0, before, :], 1, (right, up)),
        copy(right_edge.at[first_rows, :], halo.at[0, after, :], 2, (right, down)),
    ]
    go_left = [
        copy(left_edge, halo.at[1, own, :], 3, (left, lon)),
        copy(left_edge.at[last_rows, :], halo.at[1, before, :], 4, (left, up)),
        copy(left_edge.at[first_rows, :], halo.at[1, after, :], 5, (left, down)),
    ]
    go_lon = [
        copy(planes.at[:, top, :], planes.at[:, before, :], 6, (lat, up)),
        copy(planes.at[:, low, :], planes.at[:, after, :], 7, (lat, down)),
    ]

    @pl.when(has_right)
    def _():
        for c in go_right:
            c.start()

    @pl.when(has_left)
    def _():
        for c in go_left:
            c.start()

    for c in go_lon:
        c.start()

    @pl.when(lat == 0)
    def _():
        halo[0] = jnp.zeros((ext, lanes), jnp.float32)

    @pl.when(lat == nlat - 1)
    def _():
        halo[1] = jnp.zeros((ext, lanes), jnp.float32)

    for k in range(work.shape[0]):
        for s in range(2):
            work[k, s, 0:PAD, :] = jnp.zeros((PAD, lanes), jnp.float32)
            work[k, s, ext + PAD:ext + 2 * PAD, :] = jnp.zeros((PAD, lanes), jnp.float32)

    loads[3].wait()
    block = lax.broadcasted_iota(jnp.int32, (NB, lanes), 0)

    def mark(z, carry):
        hit = jnp.where(ids[pl.ds(z, 1), :] == block, 1.0, 0.0)
        hits[pl.ds(pl.multiple_of(z * NB, NB), NB), :] = hit.astype(jnp.bfloat16)
        return carry

    lax.fori_loop(0, rows, mark, 0, unroll=4)

    for c in go_lon:
        c.wait()

    @pl.when(has_left)
    def _():
        for c in go_right:
            c.wait_recv()
        for c in go_left:
            c.wait_send()

    @pl.when(has_right)
    def _():
        for c in go_left:
            c.wait_recv()
        for c in go_right:
            c.wait_send()

    chunks = [(a, min(CHUNK, ext - a)) for a in range(0, ext, CHUNK)]

    def unpack(p, a, n):
        left = pltpu.roll(halo[0, a:a + n, :], lax.rem(2 * lanes - EDGE - EDGE * p, lanes), 1)
        right = pltpu.roll(halo[1, a:a + n, :], lax.rem(2 * lanes - EDGE * p, lanes), 1)
        return jnp.where(lane < EDGE, right, jnp.where(lane >= lanes - EDGE, left, 0.0))

    for a, n in chunks:
        for s in range(2):
            if s:
                ocean, k = unpack(0, a, n), unpack(count, a, n)
            else:
                ocean, k = planes[0, a:a + n, :], planes[count, a:a + n, :]
            ocean = ocean * ocean
            coef[0, s, a:a + n, :] = ocean * (k + 0.25)
            coef[1, s, a:a + n, :] = 0.0625 * ocean

    at_first, at_last = lane == 0, lane == lanes - 1

    def apply(src, a, n, wide):
        o = a + PAD
        m, h = work[src, 0, o:o + n, :], work[src, 1, o:o + n, :]
        m_right, h_right = pltpu.roll(m, 1, 1), pltpu.roll(h, 1, 1)
        m_left, h_left = pltpu.roll(m, lanes - 1, 1), pltpu.roll(h, lanes - 1, 1)

        def one(s, x, a_side, b_side):
            total = work[src, s, o - 1:o + n - 1, :] + work[src, s, o + 1:o + n + 1, :]
            total = total + a_side + b_side
            return coef[0, s, a:a + n, :] * x - coef[1, s, a:a + n, :] * total

        out = one(0, m, jnp.where(at_first, h_right, m_right), jnp.where(at_last, h_left, m_left))
        if not wide:
            return out, None
        return out, one(
            1, h, jnp.where(at_first, m_right, h_right), jnp.where(at_last, m_left, h_left))

    def put(dst, a, n, pair):
        o = a + PAD
        work[dst, 0, o:o + n, :] = pair[0]
        work[dst, 1, o:o + n, :] = pair[1]

    def get(src, a, n):
        o = a + PAD
        return work[src, 0, o:o + n, :], work[src, 1, o:o + n, :]

    def probes(group, carry):
        each = [(u, group * GROUP + u) for u in range(GROUP)]
        for u, p in each:
            for a, n in chunks:
                put(5 * u, a, n, (planes[p, a:a + n, :], unpack(p, a, n)))
        for k in range(3):
            for u, p in each:
                for a, n in chunks:
                    put(5 * u + k + 1, a, n, apply(5 * u + k, a, n, True))
        for u, p in each:
            for a, n in chunks:
                m, h = apply(5 * u + 3, a, n, True)
                m_old, h_old = get(5 * u + 2, a, n)
                put(5 * u + 4, a, n, (m - SHIFT * m_old, h - SHIFT * h_old))
        for u, p in each:
            last_step(u, p)
        return carry

    def last_step(u, p):
        part = [jnp.zeros((8, lanes), jnp.float32) for _ in range(7)]
        step = 32
        for a in range(0, rows, step):
            w2, _ = apply(5 * u + 4, a + PAD, step, False)
            v0, w0, v1, w1, v2 = (get(5 * u + k, a + PAD, step)[0] for k in range(5))
            k = kappa[a:a + step, :]
            kept[0, p, a:a + step, :] = v1
            kept[1, p, a:a + step, :] = v2
            for j, (v, w) in enumerate(((v0, w0), (v1, w1), (v2, w2))):
                at = pl.ds(pl.multiple_of((j * count + p) * rows + a, 8), step)
                terms[at, :] = k * (2.0 * v0 * w0) if j == 0 else k * (v * w0 + w * v0)
            pairs = ((w0, w0), (w0, w1), (w0, w2), (w1, w1), (w1, w2), (w2, w2), (v0, v0))
            for j, (x, y) in enumerate(pairs):
                xy = x * y
                for i in range(0, step, 8):
                    part[j] = part[j] + xy[i:i + 8]
        for j in range(7):
            dots[j, pl.ds(p, 1), :] = jnp.sum(part[j], axis=0, keepdims=True)

    lax.fori_loop(0, count // GROUP, probes, 0)

    def share(buf, mine, n, send, recv, axis):
        copies = []
        for d in range(1, n):
            other = lax.rem(mine + d, n)
            source = lax.rem(mine + n - d, n)
            device = (other, lon) if axis == 0 else (lat, other)
            pltpu.make_async_remote_copy(
                src_ref=buf.at[mine], dst_ref=buf.at[mine],
                send_sem=send.at[d - 1], recv_sem=recv.at[d - 1],
                device_id=device, device_id_type=MESH).start()
            copies.append(pltpu.make_async_remote_copy(
                src_ref=buf.at[mine], dst_ref=buf.at[source],
                send_sem=send.at[d - 1], recv_sem=recv.at[d - 1],
                device_id=device, device_id_type=MESH))
        return copies

    def gather(buf, n, copies):
        for c in copies:
            c.wait()
        total = buf[0]
        for i in range(1, n):
            total = total + buf[i]
        return total

    mine = jnp.zeros((count, lanes), jnp.float32)
    for j in range(7):
        mine = jnp.where(lane == j, jnp.sum(dots[j], axis=1, keepdims=True), mine)
    gram_lat[lat] = mine
    sent = share(gram_lat, lat, nlat, lat_send.at[0], lat_recv.at[0], 0)

    def sums(step, acc):
        lhs, rhs = [], []
        for i in range(2):
            z = step * 2 + i
            x = terms[pl.ds(z, 3 * count, stride=rows), :]
            high = x.astype(jnp.bfloat16)
            low = (x - high.astype(jnp.float32)).astype(jnp.bfloat16)
            lhs.append(jnp.concatenate([high, low], axis=0))
            rhs.append(hits[pl.ds(pl.multiple_of(z * NB, NB), NB), :])
        return acc + lax.dot_general(
            jnp.concatenate(lhs, axis=1), jnp.concatenate(rhs, axis=1),
            (((1,), (1,)), ((), ())), preferred_element_type=jnp.float32)

    acc = jnp.zeros((6 * count, NB), jnp.float32)
    acc = lax.fori_loop(0, rows // 4, sums, acc, unroll=8)
    gram_lon[lon] = gather(gram_lat, nlat, sent)
    sent = share(gram_lon, lon, nlon, lon_send.at[0], lon_recv.at[0], 1)
    acc = lax.fori_loop(rows // 4, rows // 2, sums, acc, unroll=8)
    half = 3 * count // 2
    acc = acc[:3 * count] + acc[3 * count:]
    sums_lat[lat] = jnp.concatenate([acc[:half], acc[half:]], axis=1)
    sums_sent = share(sums_lat, lat, nlat, lat_send.at[1], lat_recv.at[1], 0)
    total = gather(gram_lon, nlon, sent)

    g = [total[:, j:j + 1] for j in range(7)]
    y = weights(tuple(g[:6]), (g[6], g[0], g[1] - SHIFT * g[0]))
    for j in range(3):
        ys[j] = jnp.broadcast_to(y[j], (count, lanes))
    acc = gather(sums_lat, nlat, sums_sent)
    acc = jnp.concatenate([acc[:, :NB], acc[:, NB:]], axis=0)
    local = y[0] * acc[:count] + y[1] * acc[count:2 * count] + y[2] * acc[2 * count:]
    sums_lon[lon] = jnp.concatenate([local[:count // 2], local[count // 2:]], axis=1)
    sent = share(sums_lon, lon, nlon, lon_send.at[1], lon_recv.at[1], 1)

    def finish(p, carry):
        y0, y1, y2 = (ys[j, pl.ds(p, 1), :] for j in range(3))
        solved[p] = y0 * planes[p, PAD:PAD + rows, :] + y1 * kept[0, p] + y2 * kept[1, p]
        t = [
            terms[pl.ds(pl.multiple_of((j * count + p) * rows, 8), rows), :] for j in range(3)]
        trace[p] = y0 * t[0] + y1 * t[1] + y2 * t[2]
        return carry

    stores = []
    part = count // 4
    for k in range(4):
        lax.fori_loop(k * part, (k + 1) * part, finish, 0)
        at = pl.ds(k * part, part)
        for j, (src, dst) in enumerate(((solved, solved_out), (trace, trace_out))):
            stores.append(pltpu.make_async_copy(src.at[at], dst.at[at], store_done.at[k, j]))
            stores[-1].start()
    total = gather(sums_lon, nlon, sent)
    total = jnp.concatenate([total[:, :NB], total[:, NB:]], axis=0)
    traces[...] = total / jnp.float32(rows * lanes * nlat * nlon // NB)
    for store in stores:
        store.wait()


def per_device(nlat, nlon, probe_signs, ocean_mask, kappa_sq, block_ids):
    count, rows, lanes = probe_signs.shape
    ext = rows + 2 * PAD
    f32 = jnp.float32
    vmem = pl.BlockSpec(memory_space=pltpu.VMEM)
    return pl.pallas_call(
        functools.partial(kernel, nlat, nlon),
        out_shape=(
            jax.ShapeDtypeStruct((count, rows, lanes), f32),
            jax.ShapeDtypeStruct((count, rows, lanes), f32),
            jax.ShapeDtypeStruct((count, NB), f32),
        ),
        in_specs=[pl.BlockSpec(memory_space=pltpu.HBM)] * 4,
        out_specs=(pl.BlockSpec(memory_space=pltpu.HBM),) * 2 + (vmem,),
        scratch_shapes=[
            pltpu.VMEM((count, rows, lanes), f32),
            pltpu.VMEM((count, rows, lanes), f32),
            pltpu.VMEM((count, rows, lanes), jnp.int32),
            pltpu.VMEM((rows, lanes), jnp.int32),
            pltpu.VMEM((rows, lanes), f32),
            pltpu.VMEM((rows, lanes), jnp.int32),
            pltpu.VMEM((rows * NB, lanes), jnp.bfloat16),
            pltpu.VMEM((count + 1, ext, lanes), f32),
            pltpu.VMEM((2, ext, lanes), f32),
            pltpu.VMEM((rows, lanes), f32),
            pltpu.VMEM((rows, lanes), f32),
            pltpu.VMEM((2, 2, ext, lanes), f32),
            pltpu.VMEM((5 * GROUP, 2, ext + 2 * PAD, lanes), f32),
            pltpu.VMEM((2, count, rows, lanes), f32),
            pltpu.VMEM((3 * count * rows, lanes), f32),
            pltpu.VMEM((8, count, lanes), f32),
            pltpu.VMEM((3, count, lanes), f32),
            pltpu.VMEM((nlat, count, lanes), f32),
            pltpu.VMEM((nlon, count, lanes), f32),
            pltpu.VMEM((nlat, 3 * count // 2, lanes), f32),
            pltpu.VMEM((nlon, count // 2, lanes), f32),
            pltpu.SemaphoreType.DMA((4,)),
            pltpu.SemaphoreType.DMA((4, 2)),
            pltpu.SemaphoreType.DMA((8,)),
            pltpu.SemaphoreType.DMA((8,)),
            pltpu.SemaphoreType.DMA((2, nlat - 1)),
            pltpu.SemaphoreType.DMA((2, nlat - 1)),
            pltpu.SemaphoreType.DMA((2, nlon - 1)),
            pltpu.SemaphoreType.DMA((2, nlon - 1)),
        ],
        compiler_params=pltpu.CompilerParams(
            collective_id=0, has_side_effects=True, vmem_limit_bytes=64 * 1024 * 1024),
    )(probe_signs, ocean_mask, kappa_sq, block_ids)


def solution(mesh):
    placed = (P(None, "lon", "lat"), P("lon", "lat"), P("lon", "lat"), P("lon", "lat"))
    return jax.shard_map(
        functools.partial(per_device, mesh.shape["lat"], mesh.shape["lon"]),
        mesh=mesh,
        in_specs=placed,
        out_specs=(P(None, "lon", "lat"), P(None, "lon", "lat"), P()),
        check_vma=False,
    )
```

```python
import functools

import jax
import jax.numpy as jnp
from jax import lax
from jax.experimental import pallas as pl
from jax.experimental.pallas import tpu as pltpu
from jax.sharding import PartitionSpec as P

NB = 64
EDGE = 7
PAD = 8
SHIFT = 0.4
FLOOR = 1e-6
CHUNK = 48
GROUP = 4
MESH = pl.DeviceIdType.MESH


def weights(gram, right):
    g00, g01, g02, g11, g12, g22 = gram
    r0, r1, r2 = right
    l10 = g01 / g00
    l20 = g02 / g00
    d1 = g11 - l10 * g01
    e12 = g12 - l10 * g02
    ok1 = d1 > FLOOR * g11
    i1 = jnp.where(ok1, 1.0 / jnp.where(ok1, d1, 1.0), 0.0)
    l21 = e12 * i1
    d2 = g22 - l20 * g02 - l21 * e12
    ok2 = d2 > FLOOR * g22
    i2 = jnp.where(ok2, 1.0 / jnp.where(ok2, d2, 1.0), 0.0)
    z1 = r1 - l10 * r0
    z2 = r2 - l20 * r0 - l21 * z1
    y2 = z2 * i2
    y1 = z1 * i1 - l21 * y2
    y0 = r0 / g00 - l10 * y1 - l20 * y2
    return y0, y1, y2


def kernel(
    nlat, nlon, signs_in, mask_in, kappa_in, ids_in, solved_out, trace_out, traces,
    solved, trace, signs, mask, kappa, ids, hits, planes, halo, left_edge, right_edge, coef, work, kept, terms, dots, ys,
    gram_lat, gram_lon, sums_lat, sums_lon,
    load_done, store_done, halo_send, halo_recv, lat_send, lat_recv, lon_send, lon_recv,
):
    loads = [
        pltpu.make_async_copy(src, dst, load_done.at[k])
        for k, (src, dst) in enumerate(
            ((signs_in, signs), (mask_in, mask), (kappa_in, kappa), (ids_in, ids)))]
    for load in loads:
        load.start()

    count, rows, lanes = signs.shape
    ext = rows + 2 * PAD
    lat, lon = lax.axis_index("lat"), lax.axis_index("lon")
    up, down = lax.rem(lon + 1, nlon), lax.rem(lon + nlon - 1, nlon)

    barrier = pltpu.get_barrier_semaphore()
    for d in range(1, nlat):
        pl.semaphore_signal(
            barrier, inc=1, device_id=(lax.rem(lat + d, nlat), lon), device_id_type=MESH)
    for d in range(1, nlon):
        pl.semaphore_signal(
            barrier, inc=1, device_id=(lat, lax.rem(lon + d, nlon)), device_id_type=MESH)
    has_left, has_right = lat > 0, lat < nlat - 1
    left, right = lax.max(lat - 1, 0), lax.min(lat + 1, nlat - 1)
    for there, side in ((has_left, left), (has_right, right)):
        @pl.when(there)
        def _(side=side):
            for end in (up, down):
                pl.semaphore_signal(
                    barrier, inc=1, device_id=(side, end), device_id_type=MESH)

    for load in loads[:3]:
        load.wait()
    lane = lax.broadcasted_iota(jnp.int32, (1, lanes), 1)

    def pack(step, carry):
        part = pl.ds(pl.multiple_of(step * 32, 32), 32)
        ocean = mask[part, :].astype(jnp.float32)
        first = jnp.zeros((32, lanes), jnp.float32)
        last = jnp.zeros((32, lanes), jnp.float32)
        for p in range(count + 1):
            if p < count:
                x = signs[p, part, :].astype(jnp.float32) * ocean
            else:
                x = kappa[part, :]
            planes[p, pl.ds(pl.multiple_of(step * 32 + PAD, 8), 32), :] = x
            here = (lane >= EDGE * p) & (lane < EDGE * (p + 1))
            first = jnp.where(here, pltpu.roll(x, EDGE * p, 1) if p else x, first)
            last = jnp.where(here, pltpu.roll(x, EDGE * (p + 1), 1), last)
        left_edge[part, :] = first
        right_edge[part, :] = last
        return carry

    lax.fori_loop(0, rows // 32, pack, 0)
    sides = lax.min(lat, 1) + lax.min(nlat - 1 - lat, 1)
    pl.semaphore_wait(barrier, nlat + nlon - 2 + 2 * sides)

    def copy(src, dst, k, device):
        return pltpu.make_async_remote_copy(
            src_ref=src, dst_ref=dst, send_sem=halo_send.at[k], recv_sem=halo_recv.at[k],
            device_id=device, device_id_type=MESH)

    own = pl.ds(PAD, rows)
    top, low = pl.ds(rows, PAD), pl.ds(PAD, PAD)
    before, after = pl.ds(0, PAD), pl.ds(rows + PAD, PAD)
    first_rows, last_rows = pl.ds(0, PAD), pl.ds(rows - PAD, PAD)
    go_right = [
        copy(right_edge, halo.at[0, own, :], 0, (right, lon)),
        copy(right_edge.at[last_rows, :], halo.at[0, before, :], 1, (right, up)),
        copy(right_edge.at[first_rows, :], halo.at[0, after, :], 2, (right, down)),
    ]
    go_left = [
        copy(left_edge, halo.at[1, own, :], 3, (left, lon)),
        copy(left_edge.at[last_rows, :], halo.at[1, before, :], 4, (left, up)),
        copy(left_edge.at[first_rows, :], halo.at[1, after, :], 5, (left, down)),
    ]
    go_lon = [
        copy(planes.at[:, top, :], planes.at[:, before, :], 6, (lat, up)),
        copy(planes.at[:, low, :], planes.at[:, after, :], 7, (lat, down)),
    ]

    @pl.when(has_right)
    def _():
        for c in go_right:
            c.start()

    @pl.when(has_left)
    def _():
        for c in go_left:
            c.start()

    for c in go_lon:
        c.start()

    @pl.when(lat == 0)
    def _():
        halo[0] = jnp.zeros((ext, lanes), jnp.float32)

    @pl.when(lat == nlat - 1)
    def _():
        halo[1] = jnp.zeros((ext, lanes), jnp.float32)

    for k in range(work.shape[0]):
        for s in range(2):
            work[k, s, 0:PAD, :] = jnp.zeros((PAD, lanes), jnp.float32)
            work[k, s, ext + PAD:ext + 2 * PAD, :] = jnp.zeros((PAD, lanes), jnp.float32)

    loads[3].wait()
    block = lax.broadcasted_iota(jnp.int32, (NB, lanes), 0)

    def mark(z, carry):
        hit = jnp.where(ids[pl.ds(z, 1), :] == block, 1.0, 0.0)
        hits[pl.ds(pl.multiple_of(z * NB, NB), NB), :] = hit.astype(jnp.bfloat16)
        return carry

    lax.fori_loop(0, rows, mark, 0, unroll=4)

    for c in go_lon:
        c.wait()

    @pl.when(has_left)
    def _():
        for c in go_right:
            c.wait_recv()
        for c in go_left:
            c.wait_send()

    @pl.when(has_right)
    def _():
        for c in go_left:
            c.wait_recv()
        for c in go_right:
            c.wait_send()

    chunks = [(a, min(CHUNK, ext - a)) for a in range(0, ext, CHUNK)]

    width = lanes // GROUP
    spot = lax.rem(lane, width)

    def strip(pairs, a, n):
        out = jnp.zeros((n, lanes), jnp.float32)
        for u, p in pairs:
            x = planes[p, a:a + n, :]
            pieces = (
                (x, width * u + 8, 0, 8),
                (halo[1, a:a + n, :], lax.rem(width * u + 8 - EDGE * p + 2 * lanes, lanes), 8, 15),
                (halo[0, a:a + n, :], lax.rem(width * u + 17 - EDGE * p + 2 * lanes, lanes), 17, 24),
                (x, (width * u + 24) % lanes, 24, 32),
            )
            for source, shift, lo, hi in pieces:
                here = (lane >= width * u + lo) & (lane < width * u + hi)
                out = jnp.where(here, pltpu.roll(source, shift, 1), out)
        return out

    for a, n in chunks:
        for s in range(2):
            if s:
                ocean = strip([(u, 0) for u in range(GROUP)], a, n)
                k = strip([(u, count) for u in range(GROUP)], a, n)
            else:
                ocean, k = planes[0, a:a + n, :], planes[count, a:a + n, :]
            ocean = ocean * ocean
            coef[0, s, a:a + n, :] = ocean * (k + 0.25)
            coef[1, s, a:a + n, :] = 0.0625 * ocean

    at_first, at_last = lane == 0, lane == lanes - 1

    def vertical(src, s, o, n):
        return work[src, s, o - 1:o + n - 1, :] + work[src, s, o + 1:o + n + 1, :]

    def apply(u, k, a, n):
        o, src = a + PAD, 5 * u + k
        m = work[src, 0, o:o + n, :]
        e = pltpu.roll(work[5 + k, 1, o:o + n, :], (2 * lanes - width * u - 23) % lanes, 1)
        total = vertical(src, 0, o, n) + jnp.where(at_first, e, pltpu.roll(m, 1, 1))
        total = total + jnp.where(at_last, e, pltpu.roll(m, lanes - 1, 1))
        return coef[0, 0, a:a + n, :] * m - coef[1, 0, a:a + n, :] * total

    def apply_strip(k, a, n):
        o = a + PAD
        x = work[k, 1, o:o + n, :]
        total = vertical(k, 1, o, n) + pltpu.roll(x, 1, 1) + pltpu.roll(x, lanes - 1, 1)
        return coef[0, 1, a:a + n, :] * x - coef[1, 1, a:a + n, :] * total

    def put_strip(k, a, n, x):
        o = a + PAD
        work[k, 1, o:o + n, :] = x
        work[5 + k, 1, o:o + n, :] = jnp.where(spot == 23, x, pltpu.roll(x, 14, 1))

    def get(src, a, n):
        return work[src, 0, a + PAD:a + PAD + n, :]

    def probes(group, carry):
        each = [(u, group * GROUP + u) for u in range(GROUP)]
        for a, n in chunks:
            put_strip(0, a, n, strip(each, a, n))
            for u, p in each:
                work[5 * u, 0, a + PAD:a + PAD + n, :] = planes[p, a:a + n, :]
        for k in range(4):
            for a, n in chunks:
                x = apply_strip(k, a, n)
                if k == 3:
                    x = x - SHIFT * work[2, 1, a + PAD:a + PAD + n, :]
                put_strip(k + 1, a, n, x)
            for u, p in each:
                for a, n in chunks:
                    x = apply(u, k, a, n)
                    if k == 3:
                        x = x - SHIFT * get(5 * u + 2, a, n)
                    work[5 * u + k + 1, 0, a + PAD:a + PAD + n, :] = x
        for u, p in each:
            last_step(u, p)
        return carry

    def last_step(u, p):
        part = [jnp.zeros((8, lanes), jnp.float32) for _ in range(7)]
        step = 32
        for a in range(0, rows, step):
            w2 = apply(u, 4, a + PAD, step)
            v0, w0, v1, w1, v2 = (get(5 * u + k, a + PAD, step) for k in range(5))
            k = kappa[a:a + step, :]
            kept[0, p, a:a + step, :] = v1
            kept[1, p, a:a + step, :] = v2
            for j, (v, w) in enumerate(((v0, w0), (v1, w1), (v2, w2))):
                at = pl.ds(pl.multiple_of((j * count + p) * rows + a, 8), step)
                terms[at, :] = k * (2.0 * v0 * w0) if j == 0 else k * (v * w0 + w * v0)
            pairs = ((w0, w0), (w0, w1), (w0, w2), (w1, w1), (w1, w2), (w2, w2), (v0, v0))
            for j, (x, y) in enumerate(pairs):
                xy = x * y
                for i in range(0, step, 8):
                    part[j] = part[j] + xy[i:i + 8]
        for j in range(7):
            dots[j, pl.ds(p, 1), :] = jnp.sum(part[j], axis=0, keepdims=True)

    lax.fori_loop(0, count // GROUP, probes, 0)

    def share(buf, mine, n, send, recv, axis):
        copies = []
        for d in range(1, n):
            other = lax.rem(mine + d, n)
            source = lax.rem(mine + n - d, n)
            device = (other, lon) if axis == 0 else (lat, other)
            pltpu.make_async_remote_copy(
                src_ref=buf.at[mine], dst_ref=buf.at[mine],
                send_sem=send.at[d - 1], recv_sem=recv.at[d - 1],
                device_id=device, device_id_type=MESH).start()
            copies.append(pltpu.make_async_remote_copy(
                src_ref=buf.at[mine], dst_ref=buf.at[source],
                send_sem=send.at[d - 1], recv_sem=recv.at[d - 1],
                device_id=device, device_id_type=MESH))
        return copies

    def gather(buf, n, copies):
        for c in copies:
            c.wait()
        total = buf[0]
        for i in range(1, n):
            total = total + buf[i]
        return total

    mine = jnp.zeros((count, lanes), jnp.float32)
    for j in range(7):
        mine = jnp.where(lane == j, jnp.sum(dots[j], axis=1, keepdims=True), mine)
    gram_lat[lat] = mine
    sent = share(gram_lat, lat, nlat, lat_send.at[0], lat_recv.at[0], 0)

    def sums(step, acc):
        lhs, rhs = [], []
        for i in range(2):
            z = step * 2 + i
            x = terms[pl.ds(z, 3 * count, stride=rows), :]
            high = x.astype(jnp.bfloat16)
            low = (x - high.astype(jnp.float32)).astype(jnp.bfloat16)
            lhs.append(jnp.concatenate([high, low], axis=0))
            rhs.append(hits[pl.ds(pl.multiple_of(z * NB, NB), NB), :])
        return acc + lax.dot_general(
            jnp.concatenate(lhs, axis=1), jnp.concatenate(rhs, axis=1),
            (((1,), (1,)), ((), ())), preferred_element_type=jnp.float32)

    acc = jnp.zeros((6 * count, NB), jnp.float32)
    acc = lax.fori_loop(0, rows // 4, sums, acc, unroll=8)
    gram_lon[lon] = gather(gram_lat, nlat, sent)
    sent = share(gram_lon, lon, nlon, lon_send.at[0], lon_recv.at[0], 1)
    acc = lax.fori_loop(rows // 4, rows // 2, sums, acc, unroll=8)
    half = 3 * count // 2
    acc = acc[:3 * count] + acc[3 * count:]
    sums_lat[lat] = jnp.concatenate([acc[:half], acc[half:]], axis=1)
    sums_sent = share(sums_lat, lat, nlat, lat_send.at[1], lat_recv.at[1], 0)
    total = gather(gram_lon, nlon, sent)

    g = [total[:, j:j + 1] for j in range(7)]
    y = weights(tuple(g[:6]), (g[6], g[0], g[1] - SHIFT * g[0]))
    for j in range(3):
        ys[j] = jnp.broadcast_to(y[j], (count, lanes))
    acc = gather(sums_lat, nlat, sums_sent)
    acc = jnp.concatenate([acc[:, :NB], acc[:, NB:]], axis=0)
    local = y[0] * acc[:count] + y[1] * acc[count:2 * count] + y[2] * acc[2 * count:]
    sums_lon[lon] = jnp.concatenate([local[:count // 2], local[count // 2:]], axis=1)
    sent = share(sums_lon, lon, nlon, lon_send.at[1], lon_recv.at[1], 1)

    def finish(p, carry):
        y0, y1, y2 = (ys[j, pl.ds(p, 1), :] for j in range(3))
        solved[p] = y0 * planes[p, PAD:PAD + rows, :] + y1 * kept[0, p] + y2 * kept[1, p]
        t = [
            terms[pl.ds(pl.multiple_of((j * count + p) * rows, 8), rows), :] for j in range(3)]
        trace[p] = y0 * t[0] + y1 * t[1] + y2 * t[2]
        return carry

    stores = []
    part = count // 4
    for k in range(4):
        lax.fori_loop(k * part, (k + 1) * part, finish, 0)
        at = pl.ds(k * part, part)
        for j, (src, dst) in enumerate(((solved, solved_out), (trace, trace_out))):
            stores.append(pltpu.make_async_copy(src.at[at], dst.at[at], store_done.at[k, j]))
            stores[-1].start()
    total = gather(sums_lon, nlon, sent)
    total = jnp.concatenate([total[:, :NB], total[:, NB:]], axis=0)
    traces[...] = total / jnp.float32(rows * lanes * nlat * nlon // NB)
    for store in stores:
        store.wait()


def per_device(nlat, nlon, probe_signs, ocean_mask, kappa_sq, block_ids):
    count, rows, lanes = probe_signs.shape
    ext = rows + 2 * PAD
    f32 = jnp.float32
    vmem = pl.BlockSpec(memory_space=pltpu.VMEM)
    return pl.pallas_call(
        functools.partial(kernel, nlat, nlon),
        out_shape=(
            jax.ShapeDtypeStruct((count, rows, lanes), f32),
            jax.ShapeDtypeStruct((count, rows, lanes), f32),
            jax.ShapeDtypeStruct((count, NB), f32),
        ),
        in_specs=[pl.BlockSpec(memory_space=pltpu.HBM)] * 4,
        out_specs=(pl.BlockSpec(memory_space=pltpu.HBM),) * 2 + (vmem,),
        scratch_shapes=[
            pltpu.VMEM((count, rows, lanes), f32),
            pltpu.VMEM((count, rows, lanes), f32),
            pltpu.VMEM((count, rows, lanes), jnp.int32),
            pltpu.VMEM((rows, lanes), jnp.int32),
            pltpu.VMEM((rows, lanes), f32),
            pltpu.VMEM((rows, lanes), jnp.int32),
            pltpu.VMEM((rows * NB, lanes), jnp.bfloat16),
            pltpu.VMEM((count + 1, ext, lanes), f32),
            pltpu.VMEM((2, ext, lanes), f32),
            pltpu.VMEM((rows, lanes), f32),
            pltpu.VMEM((rows, lanes), f32),
            pltpu.VMEM((2, 2, ext, lanes), f32),
            pltpu.VMEM((5 * GROUP, 2, ext + 2 * PAD, lanes), f32),
            pltpu.VMEM((2, count, rows, lanes), f32),
            pltpu.VMEM((3 * count * rows, lanes), f32),
            pltpu.VMEM((8, count, lanes), f32),
            pltpu.VMEM((3, count, lanes), f32),
            pltpu.VMEM((nlat, count, lanes), f32),
            pltpu.VMEM((nlon, count, lanes), f32),
            pltpu.VMEM((nlat, 3 * count // 2, lanes), f32),
            pltpu.VMEM((nlon, count // 2, lanes), f32),
            pltpu.SemaphoreType.DMA((4,)),
            pltpu.SemaphoreType.DMA((4, 2)),
            pltpu.SemaphoreType.DMA((8,)),
            pltpu.SemaphoreType.DMA((8,)),
            pltpu.SemaphoreType.DMA((2, nlat - 1)),
            pltpu.SemaphoreType.DMA((2, nlat - 1)),
            pltpu.SemaphoreType.DMA((2, nlon - 1)),
            pltpu.SemaphoreType.DMA((2, nlon - 1)),
        ],
        compiler_params=pltpu.CompilerParams(
            collective_id=0, has_side_effects=True, vmem_limit_bytes=64 * 1024 * 1024),
    )(probe_signs, ocean_mask, kappa_sq, block_ids)


def solution(mesh):
    placed = (P(None, "lon", "lat"), P("lon", "lat"), P("lon", "lat"), P("lon", "lat"))
    return jax.shard_map(
        functools.partial(per_device, mesh.shape["lat"], mesh.shape["lon"]),
        mesh=mesh,
        in_specs=placed,
        out_specs=(P(None, "lon", "lat"), P(None, "lon", "lat"), P()),
        check_vma=False,
    )
```

```python
import functools

import jax
import jax.numpy as jnp
from jax import lax
from jax.experimental import pallas as pl
from jax.experimental.pallas import tpu as pltpu
from jax.sharding import PartitionSpec as P

NB = 64
EDGE = 7
PAD = 8
SHIFT = 0.4
FLOOR = 1e-6
CHUNK = 24
GROUP = 4
MESH = pl.DeviceIdType.MESH


def weights(gram, right):
    g00, g01, g02, g11, g12, g22 = gram
    r0, r1, r2 = right
    l10 = g01 / g00
    l20 = g02 / g00
    d1 = g11 - l10 * g01
    e12 = g12 - l10 * g02
    ok1 = d1 > FLOOR * g11
    i1 = jnp.where(ok1, 1.0 / jnp.where(ok1, d1, 1.0), 0.0)
    l21 = e12 * i1
    d2 = g22 - l20 * g02 - l21 * e12
    ok2 = d2 > FLOOR * g22
    i2 = jnp.where(ok2, 1.0 / jnp.where(ok2, d2, 1.0), 0.0)
    z1 = r1 - l10 * r0
    z2 = r2 - l20 * r0 - l21 * z1
    y2 = z2 * i2
    y1 = z1 * i1 - l21 * y2
    y0 = r0 / g00 - l10 * y1 - l20 * y2
    return y0, y1, y2


def kernel(
    nlat, nlon, signs_in, mask_in, kappa_in, ids_in, solved_out, trace_out, traces,
    solved, trace, signs, mask, kappa, ids, hits, planes, halo, left_edge, right_edge, coef, work, kept, terms, dots, ys,
    gram_lat, gram_lon, sums_lat, sums_lon,
    load_done, store_done, halo_send, halo_recv, lat_send, lat_recv, lon_send, lon_recv,
):
    loads = [
        pltpu.make_async_copy(src, dst, load_done.at[k])
        for k, (src, dst) in enumerate(
            ((signs_in, signs), (mask_in, mask), (kappa_in, kappa), (ids_in, ids)))]
    for load in loads:
        load.start()

    count, rows, lanes = signs.shape
    ext = rows + 2 * PAD
    lat, lon = lax.axis_index("lat"), lax.axis_index("lon")
    up, down = lax.rem(lon + 1, nlon), lax.rem(lon + nlon - 1, nlon)

    barrier = pltpu.get_barrier_semaphore()
    for d in range(1, nlat):
        pl.semaphore_signal(
            barrier, inc=1, device_id=(lax.rem(lat + d, nlat), lon), device_id_type=MESH)
    for d in range(1, nlon):
        pl.semaphore_signal(
            barrier, inc=1, device_id=(lat, lax.rem(lon + d, nlon)), device_id_type=MESH)
    has_left, has_right = lat > 0, lat < nlat - 1
    left, right = lax.max(lat - 1, 0), lax.min(lat + 1, nlat - 1)
    for there, side in ((has_left, left), (has_right, right)):
        @pl.when(there)
        def _(side=side):
            for end in (up, down):
                pl.semaphore_signal(
                    barrier, inc=1, device_id=(side, end), device_id_type=MESH)

    for load in loads[:3]:
        load.wait()
    lane = lax.broadcasted_iota(jnp.int32, (1, lanes), 1)

    def pack(step, carry):
        part = pl.ds(pl.multiple_of(step * 32, 32), 32)
        ocean = mask[part, :].astype(jnp.float32)
        first = jnp.zeros((32, lanes), jnp.float32)
        last = jnp.zeros((32, lanes), jnp.float32)
        for p in range(count + 1):
            if p < count:
                x = signs[p, part, :].astype(jnp.float32) * ocean
            else:
                x = kappa[part, :]
            planes[p, pl.ds(pl.multiple_of(step * 32 + PAD, 8), 32), :] = x
            here = (lane >= EDGE * p) & (lane < EDGE * (p + 1))
            first = jnp.where(here, pltpu.roll(x, EDGE * p, 1) if p else x, first)
            last = jnp.where(here, pltpu.roll(x, EDGE * (p + 1), 1), last)
        left_edge[part, :] = first
        right_edge[part, :] = last
        return carry

    lax.fori_loop(0, rows // 32, pack, 0)
    sides = lax.min(lat, 1) + lax.min(nlat - 1 - lat, 1)
    pl.semaphore_wait(barrier, nlat + nlon - 2 + 2 * sides)

    def copy(src, dst, k, device):
        return pltpu.make_async_remote_copy(
            src_ref=src, dst_ref=dst, send_sem=halo_send.at[k], recv_sem=halo_recv.at[k],
            device_id=device, device_id_type=MESH)

    own = pl.ds(PAD, rows)
    top, low = pl.ds(rows, PAD), pl.ds(PAD, PAD)
    before, after = pl.ds(0, PAD), pl.ds(rows + PAD, PAD)
    first_rows, last_rows = pl.ds(0, PAD), pl.ds(rows - PAD, PAD)
    go_right = [
        copy(right_edge, halo.at[0, own, :], 0, (right, lon)),
        copy(right_edge.at[last_rows, :], halo.at[0, before, :], 1, (right, up)),
        copy(right_edge.at[first_rows, :], halo.at[0, after, :], 2, (right, down)),
    ]
    go_left = [
        copy(left_edge, halo.at[1, own, :], 3, (left, lon)),
        copy(left_edge.at[last_rows, :], halo.at[1, before, :], 4, (left, up)),
        copy(left_edge.at[first_rows, :], halo.at[1, after, :], 5, (left, down)),
    ]
    go_lon = [
        copy(planes.at[:, top, :], planes.at[:, before, :], 6, (lat, up)),
        copy(planes.at[:, low, :], planes.at[:, after, :], 7, (lat, down)),
    ]

    @pl.when(has_right)
    def _():
        for c in go_right:
            c.start()

    @pl.when(has_left)
    def _():
        for c in go_left:
            c.start()

    for c in go_lon:
        c.start()

    @pl.when(lat == 0)
    def _():
        halo[0] = jnp.zeros((ext, lanes), jnp.float32)

    @pl.when(lat == nlat - 1)
    def _():
        halo[1] = jnp.zeros((ext, lanes), jnp.float32)

    for k in range(work.shape[0]):
        for s in range(2):
            work[k, s, 0:PAD, :] = jnp.zeros((PAD, lanes), jnp.float32)
            work[k, s, ext + PAD:ext + 2 * PAD, :] = jnp.zeros((PAD, lanes), jnp.float32)

    loads[3].wait()
    block = lax.broadcasted_iota(jnp.int32, (NB, lanes), 0)

    def mark(z, carry):
        hit = jnp.where(ids[pl.ds(z, 1), :] == block, 1.0, 0.0)
        hits[pl.ds(pl.multiple_of(z * NB, NB), NB), :] = hit.astype(jnp.bfloat16)
        return carry

    lax.fori_loop(0, rows, mark, 0, unroll=4)

    for c in go_lon:
        c.wait()

    @pl.when(has_left)
    def _():
        for c in go_right:
            c.wait_recv()
        for c in go_left:
            c.wait_send()

    @pl.when(has_right)
    def _():
        for c in go_left:
            c.wait_recv()
        for c in go_right:
            c.wait_send()

    chunks = [(a, min(CHUNK, ext - a)) for a in range(0, ext, CHUNK)]

    def unpack(p, a, n):
        left = pltpu.roll(halo[0, a:a + n, :], lax.rem(2 * lanes - EDGE - EDGE * p, lanes), 1)
        right = pltpu.roll(halo[1, a:a + n, :], lax.rem(2 * lanes - EDGE * p, lanes), 1)
        return jnp.where(lane < EDGE, right, jnp.where(lane >= lanes - EDGE, left, 0.0))

    for a, n in chunks:
        for s in range(2):
            if s:
                ocean, k = unpack(0, a, n), unpack(count, a, n)
            else:
                ocean, k = planes[0, a:a + n, :], planes[count, a:a + n, :]
            ocean = ocean * ocean
            coef[0, s, a:a + n, :] = ocean * (k + 0.25)
            coef[1, s, a:a + n, :] = 0.0625 * ocean

    at_first, at_last = lane == 0, lane == lanes - 1

    def apply(src, a, n, wide):
        o = a + PAD
        m, h = work[src, 0, o:o + n, :], work[src, 1, o:o + n, :]
        m_right, h_right = pltpu.roll(m, 1, 1), pltpu.roll(h, 1, 1)
        m_left, h_left = pltpu.roll(m, lanes - 1, 1), pltpu.roll(h, lanes - 1, 1)

        def one(s, x, a_side, b_side):
            total = work[src, s, o - 1:o + n - 1, :] + work[src, s, o + 1:o + n + 1, :]
            total = total + a_side + b_side
            return coef[0, s, a:a + n, :] * x - coef[1, s, a:a + n, :] * total

        out = one(0, m, jnp.where(at_first, h_right, m_right), jnp.where(at_last, h_left, m_left))
        if not wide:
            return out, None
        return out, one(
            1, h, jnp.where(at_first, m_right, h_right), jnp.where(at_last, m_left, h_left))

    def put(dst, a, n, pair):
        o = a + PAD
        work[dst, 0, o:o + n, :] = pair[0]
        work[dst, 1, o:o + n, :] = pair[1]

    def get(src, a, n):
        o = a + PAD
        return work[src, 0, o:o + n, :], work[src, 1, o:o + n, :]

    def probes(group, carry):
        each = [(u, group * GROUP + u) for u in range(GROUP)]
        for u, p in each:
            for a, n in chunks:
                put(5 * u, a, n, (planes[p, a:a + n, :], unpack(p, a, n)))
        for k in range(3):
            for u, p in each:
                for a, n in chunks:
                    put(5 * u + k + 1, a, n, apply(5 * u + k, a, n, True))
        for u, p in each:
            for a, n in chunks:
                m, h = apply(5 * u + 3, a, n, True)
                m_old, h_old = get(5 * u + 2, a, n)
                put(5 * u + 4, a, n, (m - SHIFT * m_old, h - SHIFT * h_old))
        for u, p in each:
            last_step(u, p)
        return carry

    def last_step(u, p):
        part = [jnp.zeros((8, lanes), jnp.float32) for _ in range(7)]
        step = 32
        for a in range(0, rows, step):
            w2, _ = apply(5 * u + 4, a + PAD, step, False)
            v0, w0, v1, w1, v2 = (get(5 * u + k, a + PAD, step)[0] for k in range(5))
            k = kappa[a:a + step, :]
            kept[0, p, a:a + step, :] = v1
            kept[1, p, a:a + step, :] = v2
            for j, (v, w) in enumerate(((v0, w0), (v1, w1), (v2, w2))):
                at = pl.ds(pl.multiple_of((j * count + p) * rows + a, 8), step)
                terms[at, :] = k * (2.0 * v0 * w0) if j == 0 else k * (v * w0 + w * v0)
            pairs = ((w0, w0), (w0, w1), (w0, w2), (w1, w1), (w1, w2), (w2, w2), (v0, v0))
            for j, (x, y) in enumerate(pairs):
                xy = x * y
                for i in range(0, step, 8):
                    part[j] = part[j] + xy[i:i + 8]
        for j in range(7):
            dots[j, pl.ds(p, 1), :] = jnp.sum(part[j], axis=0, keepdims=True)

    lax.fori_loop(0, count // GROUP, probes, 0)

    def share(buf, mine, n, send, recv, axis):
        copies = []
        for d in range(1, n):
            other = lax.rem(mine + d, n)
            source = lax.rem(mine + n - d, n)
            device = (other, lon) if axis == 0 else (lat, other)
            pltpu.make_async_remote_copy(
                src_ref=buf.at[mine], dst_ref=buf.at[mine],
                send_sem=send.at[d - 1], recv_sem=recv.at[d - 1],
                device_id=device, device_id_type=MESH).start()
            copies.append(pltpu.make_async_remote_copy(
                src_ref=buf.at[mine], dst_ref=buf.at[source],
                send_sem=send.at[d - 1], recv_sem=recv.at[d - 1],
                device_id=device, device_id_type=MESH))
        return copies

    def gather(buf, n, copies):
        for c in copies:
            c.wait()
        total = buf[0]
        for i in range(1, n):
            total = total + buf[i]
        return total

    mine = jnp.zeros((count, lanes), jnp.float32)
    for j in range(7):
        mine = jnp.where(lane == j, jnp.sum(dots[j], axis=1, keepdims=True), mine)
    gram_lat[lat] = mine
    sent = share(gram_lat, lat, nlat, lat_send.at[0], lat_recv.at[0], 0)

    def sums(step, acc):
        lhs, rhs = [], []
        for i in range(2):
            z = step * 2 + i
            x = terms[pl.ds(z, 3 * count, stride=rows), :]
            high = x.astype(jnp.bfloat16)
            low = (x - high.astype(jnp.float32)).astype(jnp.bfloat16)
            lhs.append(jnp.concatenate([high, low], axis=0))
            rhs.append(hits[pl.ds(pl.multiple_of(z * NB, NB), NB), :])
        return acc + lax.dot_general(
            jnp.concatenate(lhs, axis=1), jnp.concatenate(rhs, axis=1),
            (((1,), (1,)), ((), ())), preferred_element_type=jnp.float32)

    acc = jnp.zeros((6 * count, NB), jnp.float32)
    acc = lax.fori_loop(0, rows // 4, sums, acc, unroll=8)
    gram_lon[lon] = gather(gram_lat, nlat, sent)
    sent = share(gram_lon, lon, nlon, lon_send.at[0], lon_recv.at[0], 1)
    acc = lax.fori_loop(rows // 4, rows // 2, sums, acc, unroll=8)
    half = 3 * count // 2
    acc = acc[:3 * count] + acc[3 * count:]
    sums_lat[lat] = jnp.concatenate([acc[:half], acc[half:]], axis=1)
    sums_sent = share(sums_lat, lat, nlat, lat_send.at[1], lat_recv.at[1], 0)
    total = gather(gram_lon, nlon, sent)

    g = [total[:, j:j + 1] for j in range(7)]
    y = weights(tuple(g[:6]), (g[6], g[0], g[1] - SHIFT * g[0]))
    for j in range(3):
        ys[j] = jnp.broadcast_to(y[j], (count, lanes))
    acc = gather(sums_lat, nlat, sums_sent)
    acc = jnp.concatenate([acc[:, :NB], acc[:, NB:]], axis=0)
    local = y[0] * acc[:count] + y[1] * acc[count:2 * count] + y[2] * acc[2 * count:]
    sums_lon[lon] = jnp.concatenate([local[:count // 2], local[count // 2:]], axis=1)
    sent = share(sums_lon, lon, nlon, lon_send.at[1], lon_recv.at[1], 1)

    def finish(p, carry):
        y0, y1, y2 = (ys[j, pl.ds(p, 1), :] for j in range(3))
        solved[p] = y0 * planes[p, PAD:PAD + rows, :] + y1 * kept[0, p] + y2 * kept[1, p]
        t = [
            terms[pl.ds(pl.multiple_of((j * count + p) * rows, 8), rows), :] for j in range(3)]
        trace[p] = y0 * t[0] + y1 * t[1] + y2 * t[2]
        return carry

    stores = []
    part = count // 4
    for k in range(4):
        lax.fori_loop(k * part, (k + 1) * part, finish, 0)
        at = pl.ds(k * part, part)
        for j, (src, dst) in enumerate(((solved, solved_out), (trace, trace_out))):
            stores.append(pltpu.make_async_copy(src.at[at], dst.at[at], store_done.at[k, j]))
            stores[-1].start()
    total = gather(sums_lon, nlon, sent)
    total = jnp.concatenate([total[:, :NB], total[:, NB:]], axis=0)
    traces[...] = total / jnp.float32(rows * lanes * nlat * nlon // NB)
    for store in stores:
        store.wait()


def per_device(nlat, nlon, probe_signs, ocean_mask, kappa_sq, block_ids):
    count, rows, lanes = probe_signs.shape
    ext = rows + 2 * PAD
    f32 = jnp.float32
    vmem = pl.BlockSpec(memory_space=pltpu.VMEM)
    return pl.pallas_call(
        functools.partial(kernel, nlat, nlon),
        out_shape=(
            jax.ShapeDtypeStruct((count, rows, lanes), f32),
            jax.ShapeDtypeStruct((count, rows, lanes), f32),
            jax.ShapeDtypeStruct((count, NB), f32),
        ),
        in_specs=[pl.BlockSpec(memory_space=pltpu.HBM)] * 4,
        out_specs=(pl.BlockSpec(memory_space=pltpu.HBM),) * 2 + (vmem,),
        scratch_shapes=[
            pltpu.VMEM((count, rows, lanes), f32),
            pltpu.VMEM((count, rows, lanes), f32),
            pltpu.VMEM((count, rows, lanes), jnp.int32),
            pltpu.VMEM((rows, lanes), jnp.int32),
            pltpu.VMEM((rows, lanes), f32),
            pltpu.VMEM((rows, lanes), jnp.int32),
            pltpu.VMEM((rows * NB, lanes), jnp.bfloat16),
            pltpu.VMEM((count + 1, ext, lanes), f32),
            pltpu.VMEM((2, ext, lanes), f32),
            pltpu.VMEM((rows, lanes), f32),
            pltpu.VMEM((rows, lanes), f32),
            pltpu.VMEM((2, 2, ext, lanes), f32),
            pltpu.VMEM((5 * GROUP, 2, ext + 2 * PAD, lanes), f32),
            pltpu.VMEM((2, count, rows, lanes), f32),
            pltpu.VMEM((3 * count * rows, lanes), f32),
            pltpu.VMEM((8, count, lanes), f32),
            pltpu.VMEM((3, count, lanes), f32),
            pltpu.VMEM((nlat, count, lanes), f32),
            pltpu.VMEM((nlon, count, lanes), f32),
            pltpu.VMEM((nlat, 3 * count // 2, lanes), f32),
            pltpu.VMEM((nlon, count // 2, lanes), f32),
            pltpu.SemaphoreType.DMA((4,)),
            pltpu.SemaphoreType.DMA((4, 2)),
            pltpu.SemaphoreType.DMA((8,)),
            pltpu.SemaphoreType.DMA((8,)),
            pltpu.SemaphoreType.DMA((2, nlat - 1)),
            pltpu.SemaphoreType.DMA((2, nlat - 1)),
            pltpu.SemaphoreType.DMA((2, nlon - 1)),
            pltpu.SemaphoreType.DMA((2, nlon - 1)),
        ],
        compiler_params=pltpu.CompilerParams(
            collective_id=0, has_side_effects=True, vmem_limit_bytes=64 * 1024 * 1024),
    )(probe_signs, ocean_mask, kappa_sq, block_ids)


def solution(mesh):
    placed = (P(None, "lon", "lat"), P("lon", "lat"), P("lon", "lat"), P("lon", "lat"))
    return jax.shard_map(
        functools.partial(per_device, mesh.shape["lat"], mesh.shape["lon"]),
        mesh=mesh,
        in_specs=placed,
        out_specs=(P(None, "lon", "lat"), P(None, "lon", "lat"), P()),
        check_vma=False,
    )
```
